512 devices in a mesh: ctx: 64 (over z, y), head: 8 (over x, core).
Axes of the slice: x: 4, y: 4, z: 16, core: 2. Of those that a mesh axis runs over, the one named last changes fastest.
Arguments:
- queries: bfloat16 [65536, 2048], P(('ctx', 'head')), may hold values from -240 to 240
- key_rows: bfloat16 [65536, 1024], P(('ctx', 'head')), may hold values from -6 to 6
- value_rows: bfloat16 [65536, 1024], P(('ctx', 'head')), may hold values from -6 to 6
- grad_out: bfloat16 [65536, 2048], P(('ctx', 'head')), may hold values from -6 to 6
- doc_start: int32 [65536], P('ctx'), may hold values from 0 to 65535, as said below
- reach_end: int32 [65536], P('ctx'), may hold values from 0 to 65535, as said below
Outputs:
- attended: bfloat16 [65536, 2048], P(('ctx', 'head'))
- grad_queries: bfloat16 [65536, 2048], P(('ctx', 'head'))
- grad_keys: bfloat16 [65536, 1024], P(('ctx', 'head'))
- grad_values: bfloat16 [65536, 1024], P(('ctx', 'head'))
The draws below stay inside these ranges and needn't reach their ends.
Inputs may be any that keep to these rules, and one draw needn't show every extreme that they name: Non-decreasing; doc_start[t] <= t and doc_start[t] is the position of a token whose doc_start is itself. Documents hold at most 1024 tokens, some document exactly that many; all but the last hold 256 or more. t <= reach_end[t] < t + 256, and reach_end[t] lies in t's document. Image tokens form spans of up to 256 tokens inside one document, some span exactly 256; every token of a span has the span's last position as reach_end. Each span starts fewer than 256 tokens before the end of a context shard's 1024 tokens and ends at or after that end.
All inputs are finite; a program needn't handle non-finite values.
Results may differ from the reference program's by a relative error of at most 0.03.
Values may be sent and summed in bfloat16 or wider, within the bound.
A program may use at most 128 MiB of HBM per device.

```python
import jax
import jax.numpy as jnp
from jax import lax

QH = 16
KVH = 8
HD = 128
BLK = 1024
SPAN = 256
TOKENS = 65536
N_CTX = 64


def shared_keys(key):
    base_keys = jnp.clip(jax.random.normal(key, (TOKENS, KVH, HD), jnp.float32), -6.0, 6.0)
    return base_keys


def draw_queries(key, part):
    key = jax.random.fold_in(key, 5)
    rows = jnp.clip(jax.random.normal(key, (TOKENS, QH, HD), jnp.float32), -6.0, 6.0)
    return rows.reshape(TOKENS, QH * HD).astype(jnp.bfloat16)


def draw_key_rows(key, part):
    base_keys = shared_keys(key)
    rows = base_keys
    return rows.reshape(TOKENS, KVH * HD).astype(jnp.bfloat16)


def layout(key):
    count = TOKENS // (BLK // 4) + 2
    lengths = jax.random.randint(jax.random.fold_in(key, 31), (count,), BLK // 4, BLK + 1, jnp.int32)
    lengths = lengths.at[0].set(BLK // 2)
    lengths = lengths.at[1].set(BLK)
    last_border = TOKENS - BLK
    first_ends = jnp.cumsum(lengths).astype(jnp.int32)
    nudge = jnp.where(lengths < BLK, 1, -1).astype(jnp.int32)
    lengths = jnp.where(first_ends == last_border, lengths + nudge, lengths)
    ends = jnp.cumsum(lengths).astype(jnp.int32)
    starts = ends - lengths
    place = jnp.arange(TOKENS, dtype=jnp.int32)
    which = jnp.searchsorted(ends, place, side='right').astype(jnp.int32)
    doc_first = starts[which]
    doc_last = jnp.minimum(ends[which], TOKENS) - 1
    blocks = TOKENS // BLK
    border = jnp.arange(blocks + 1, dtype=jnp.int32)
    offsets = jax.random.randint(jax.random.fold_in(key, 32), (blocks + 1,), 1, SPAN, jnp.int32)
    kept = jax.random.randint(jax.random.fold_in(key, 33), (blocks + 1,), 0, 2, jnp.int32)
    kept = jnp.where((border == 1) | (border == blocks - 1), 1, kept)
    kept = jnp.where((border == 0) | (border == blocks), 0, kept)
    span_first = border * BLK - offsets
    last_doc_first = doc_first[last_border]
    span_first = jnp.where(border == blocks - 1, jnp.maximum(span_first, last_doc_first), span_first)
    safe = jnp.clip(span_first, 0, TOKENS - 1)
    span_doc = doc_first[safe]
    span_stop = jnp.minimum(span_first + SPAN - 1, doc_last[safe])
    kept = jnp.where(span_stop >= border * BLK, kept, 0)

    def member(index):
        inside = (kept[index] == 1) & (place >= span_first[index]) & (place <= span_stop[index]) & (doc_first == span_doc[index])
        return (inside, span_stop[index])
    lower_in, lower_stop = member(place // BLK)
    upper_in, upper_stop = member(place // BLK + 1)
    reach = jnp.where(lower_in, lower_stop, jnp.where(upper_in, upper_stop, place))
    return (doc_first, reach)


def draw_doc_start(key, part):
    doc_first, reach = layout(key)
    return doc_first.astype(jnp.int32)


def draw_reach_end(key, part):
    doc_first, reach = layout(key)
    return reach.astype(jnp.int32)


def levels(key, extent, cuts, least, largest):
    factor_of = 1.0
    for position, blocks in cuts:
        heights = jax.random.uniform(jax.random.fold_in(jax.random.fold_in(key, 6), position), (blocks,), jnp.float32, least / len(cuts), largest / len(cuts))
        factor_of = factor_of * jnp.repeat(jnp.exp(heights), extent[position] // blocks).reshape((-1,) + (1,) * (len(extent) - 1 - position))
    return factor_of


def gaussian(own_key, dims, spread, most, pieces=(), held_as=jnp.bfloat16):
    loudness = levels(own_key, dims, pieces, -0.22, 0.18) if pieces else 1.0
    array = jax.random.normal(own_key, dims, jnp.float32) * spread * loudness
    return jnp.minimum(jnp.maximum(array, -most), most).astype(held_as)


def setup_inputs(seed: int = 0) -> dict:
    streams_of = jax.random.split(jax.random.key(seed), 7)
    queries = draw_queries(jax.random.fold_in(streams_of[6], 71), 0)
    key_rows = draw_key_rows(jax.random.fold_in(streams_of[6], 71), 0)
    value_rows = gaussian(streams_of[2], (TOKENS, KVH * HD), 1.0, 6.0, ((0, 512),))
    grad_out = gaussian(streams_of[3], (TOKENS, QH * HD), 1.0, 6.0, ((0, 512),))
    doc_start = draw_doc_start(jax.random.fold_in(streams_of[6], 71), 0)
    reach_end = draw_reach_end(jax.random.fold_in(streams_of[6], 71), 0)
    return dict(queries=queries, key_rows=key_rows, value_rows=value_rows, grad_out=grad_out, doc_start=doc_start, reach_end=reach_end)


query_scale = 168.0 ** -0.5


def reference(queries, key_rows, value_rows, grad_out, doc_start, reach_end):
    window = 2 * BLK + SPAN
    group = QH // KVH
    padded_keys = jnp.pad(key_rows, ((BLK, SPAN), (0, 0)))
    padded_values = jnp.pad(value_rows, ((BLK, SPAN), (0, 0)))
    zero_acc = jnp.zeros((BLK * N_CTX + BLK + SPAN, KVH * HD), jnp.float32)

    def step(carry, block):
        key_acc, value_acc = carry
        first = (block * BLK).astype(jnp.int32)
        query_f = lax.dynamic_slice_in_dim(queries, first, BLK, 0).astype(jnp.float32).reshape(BLK, KVH, group, HD)
        grad_f = lax.dynamic_slice_in_dim(grad_out, first, BLK, 0).astype(jnp.float32).reshape(BLK, KVH, group, HD)
        key_win = lax.dynamic_slice_in_dim(padded_keys, first, window, 0).astype(jnp.float32).reshape(window, KVH, HD)
        value_win = lax.dynamic_slice_in_dim(padded_values, first, window, 0).astype(jnp.float32).reshape(window, KVH, HD)
        lower = lax.dynamic_slice_in_dim(doc_start, first, BLK, 0)
        upper = lax.dynamic_slice_in_dim(reach_end, first, BLK, 0)
        key_place = first - BLK + jnp.arange(window, dtype=jnp.int32)
        allowed = (key_place[None, :] >= lower[:, None]) & (key_place[None, :] <= upper[:, None])
        scores = jnp.einsum('qhgd,khd->hgqk', query_f, key_win) * query_scale
        scores = jnp.where(allowed[None, None], scores, -jnp.inf)
        top = jnp.max(scores, axis=-1, keepdims=True)
        total = jnp.sum(jnp.exp(scores - top), axis=-1, keepdims=True)
        probs = jnp.exp(scores - (top + jnp.log(total)))
        probs_low = lax.optimization_barrier(probs.astype(jnp.bfloat16)).astype(jnp.float32)
        attended = jnp.einsum('hgqk,khd->qhgd', probs_low, value_win).astype(jnp.bfloat16)
        attended_f = lax.optimization_barrier(attended).astype(jnp.float32)
        grad_probs = jnp.einsum('qhgd,khd->hgqk', grad_f, value_win)
        delta = jnp.einsum('qhgd,qhgd->hgq', grad_f, attended_f)
        grad_scores = (query_scale * probs * (grad_probs - delta[..., None])).astype(jnp.bfloat16)
        grad_scores = lax.optimization_barrier(grad_scores).astype(jnp.float32)
        grad_query = jnp.einsum('hgqk,khd->qhgd', grad_scores, key_win).astype(jnp.bfloat16)
        key_term = jnp.einsum('hgqk,qhgd->khd', grad_scores, query_f).reshape(window, KVH * HD)
        value_term = jnp.einsum('hgqk,qhgd->khd', probs_low, grad_f).reshape(window, KVH * HD)
        key_acc = lax.dynamic_update_slice_in_dim(key_acc, lax.dynamic_slice_in_dim(key_acc, first, window, 0) + key_term, first, 0)
        value_acc = lax.dynamic_update_slice_in_dim(value_acc, lax.dynamic_slice_in_dim(value_acc, first, window, 0) + value_term, first, 0)
        return (key_acc, value_acc), (attended.reshape(BLK, QH * HD), grad_query.reshape(BLK, QH * HD))

    blocks = jnp.arange(N_CTX, dtype=jnp.int32)
    (key_acc, value_acc), (outputs, gradients) = lax.scan(step, (zero_acc, zero_acc), blocks)
    total_rows = BLK * N_CTX
    attended = outputs.reshape(total_rows, QH * HD)
    grad_queries = gradients.reshape(total_rows, QH * HD)
    grad_keys = key_acc[BLK:BLK + total_rows].astype(jnp.bfloat16)
    grad_values = value_acc[BLK:BLK + total_rows].astype(jnp.bfloat16)
    return attended, grad_queries, grad_keys, grad_values
```

```python
import jax
import jax.numpy as jnp
from jax import lax
from jax.experimental import pallas as pl
from jax.experimental.pallas import tpu as pltpu
from jax.sharding import PartitionSpec as P

HD = 128
BLK = 1024
PIECE = 128
TILE = 256
SCALE = 168.0 ** (-0.5)
SCALE_LOG2 = SCALE * 1.4426950408889634
MASKED = -1e30
MESH = pl.DeviceIdType.MESH
f32 = jnp.float32
bf16 = jnp.bfloat16


def matmul(left, right):
    return lax.dot_general(left, right, (((1,), (0,)), ((), ())), preferred_element_type=f32)


def kernel(
    q_hbm, k_hbm, v_hbm, g_hbm, lower_ref, upper_ref,
    o_hbm, gq_hbm, gk_hbm, gv_hbm,
    q_buf, g_buf, k_win, v_win, kt_win, vt_win, p_buf, dk_acc, dv_acc,
    o_buf, gq_buf, ret_send, ret_recv, own_buf,
    in_ssem, in_rsem, fwd_ssem, fwd_rsem, ahead_ssem, ahead_rsem,
    out_ssem, out_rsem, ret_ssem, ret_rsem, own_ssem, own_rsem,
):
    n_ctx = lax.axis_size("ctx")
    n = lax.axis_size("head")
    c = lax.axis_index("ctx")
    h = lax.axis_index("head")
    after = lax.rem(c + 1, n_ctx)
    before = lax.rem(c + n_ctx - 1, n_ctx)

    barrier = pltpu.get_barrier_semaphore()

    @pl.loop(1, n)
    def _(r):
        pl.semaphore_signal(barrier, inc=1, device_id=(c, lax.rem(h + r, n)), device_id_type=MESH)

    pl.semaphore_signal(barrier, inc=1, device_id=(after, h), device_id_type=MESH)
    pl.semaphore_signal(barrier, inc=1, device_id=(before, h), device_id_type=MESH)
    pl.semaphore_wait(barrier, n + 1)

    def in_src(stream, target):
        if stream < 2:
            return (k_hbm, v_hbm)[stream].at[:, pl.ds(pl.multiple_of(target * HD, HD), HD)]
        head = (stream - 2) // 2
        cols = pl.ds(pl.multiple_of(target * 2 * HD + head * HD, HD), HD)
        return (q_hbm, g_hbm)[stream % 2].at[:, cols]

    def in_dst(stream, source):
        if stream < 2:
            return (k_win, v_win)[stream].at[8 + source]
        return (q_buf, g_buf)[stream % 2].at[(stream - 2) // 2, source]

    def send_in(streams):
        for stream in streams:
            pltpu.make_async_copy(
                in_src(stream, h), in_dst(stream, h), in_rsem.at[stream, h]
            ).start()

        @pl.loop(1, n)
        def _(r):
            target = lax.rem(h + r, n)
            for stream in streams:
                pltpu.make_async_remote_copy(
                    src_ref=in_src(stream, target),
                    dst_ref=in_dst(stream, h),
                    send_sem=in_ssem.at[stream, target],
                    recv_sem=in_rsem.at[stream, h],
                    device_id=(c, target),
                    device_id_type=MESH,
                ).start()

    def wait_in(stream, source):
        dst = in_dst(stream, source)
        pltpu.make_async_copy(dst, dst, in_rsem.at[stream, source]).wait()

    def forward(side, piece):
        win = (k_win, v_win)[side]
        return pltpu.make_async_remote_copy(
            src_ref=win.at[8 + piece],
            dst_ref=win.at[piece],
            send_sem=fwd_ssem.at[side, piece],
            recv_sem=fwd_rsem.at[side, piece],
            device_id=(after, h),
            device_id_type=MESH,
        )

    def ahead(side, piece):
        win = (k_win, v_win)[side]
        return pltpu.make_async_remote_copy(
            src_ref=win.at[8 + piece],
            dst_ref=win.at[16 + piece],
            send_sem=ahead_ssem.at[side, piece],
            recv_sem=ahead_rsem.at[side, piece],
            device_id=(before, h),
            device_id_type=MESH,
        )

    send_in((0, 1))
    send_in((2, 3))

    @pl.loop(0, n)
    def _(r):
        source = lax.rem(h + n - r, n)
        for side in range(2):
            wait_in(side, source)
            forward(side, source).start()

        @pl.when(source < 2)
        def _():
            for side in range(2):
                ahead(side, source).start()

    send_in((4, 5))

    dk_acc[...] = jnp.zeros_like(dk_acc)
    dv_acc[...] = jnp.zeros_like(dv_acc)

    @pl.loop(0, 8)
    def _(piece):
        for side in range(2):
            forward(side, piece).wait_recv()

    @pl.loop(0, 2)
    def _(piece):
        for side in range(2):
            ahead(side, piece).wait_recv()

    @pl.loop(0, 9)
    def _(tile):
        rows = pl.ds(2 * tile, 2)
        kt_win[tile] = k_win[rows].reshape(TILE, HD).T
        vt_win[tile] = v_win[rows].reshape(TILE, HD).T

    place = lax.broadcasted_iota(jnp.int32, (TILE, TILE), 0)

    def block(head, i, tiles):
        rows = pl.ds(2 * i, 2)
        q = q_buf[head, rows].reshape(TILE, HD)
        g = g_buf[head, rows].reshape(TILE, HD)
        qt = q.T
        gt = g.T
        first = (c - 1) * BLK + i * TILE
        lower = lower_ref[i] - first
        upper = upper_ref[i] - first
        top = None
        for t in range(tiles):
            s = matmul(k_win[pl.ds(2 * (i + t), 2)].reshape(TILE, HD), qt) * SCALE_LOG2
            allowed = place >= lower - t * TILE
            if t >= 4:
                allowed = allowed & (place <= upper - t * TILE)
            s = jnp.where(allowed, s, MASKED)
            p_buf[t] = s
            most = jnp.max(s, axis=0, keepdims=True)
            top = most if top is None else jnp.maximum(top, most)
        total = None
        out = None
        for t in range(tiles):
            p = jnp.exp2(p_buf[t] - top)
            p_buf[t] = p
            part = jnp.sum(p, axis=0, keepdims=True)
            term = matmul(vt_win[i + t], p.astype(bf16))
            total = part if total is None else total + part
            out = term if out is None else out + term
        share = 1.0 / total
        out = (out * share).astype(bf16)
        delta = jnp.sum(gt.astype(f32) * out.astype(f32), axis=0, keepdims=True)
        o_buf[head, rows] = out.T.reshape(2, PIECE, HD)
        scaled = share * SCALE
        offset = delta * scaled
        grad_q = None
        for t in range(tiles):
            p = p_buf[t]
            dv_acc[i + t] += matmul((p * share).astype(bf16), g)
            dp = matmul(v_win[pl.ds(2 * (i + t), 2)].reshape(TILE, HD), gt)
            ds = (p * (dp * scaled - offset)).astype(bf16)
            dk_acc[i + t] += matmul(ds, q)
            term = matmul(kt_win[i + t], ds)
            grad_q = term if grad_q is None else grad_q + term
        gq_buf[head, rows] = grad_q.astype(bf16).T.reshape(2, PIECE, HD)

    def out_src(kind, head, target):
        return (o_buf, gq_buf)[kind].at[head, target]

    def out_dst(kind, head, source):
        cols = pl.ds(pl.multiple_of(source * 2 * HD + head * HD, HD), HD)
        return (o_hbm, gq_hbm)[kind].at[:, cols]

    def send_out(kind, head, target):
        @pl.when(target == h)
        def _():
            pltpu.make_async_copy(
                out_src(kind, head, target), out_dst(kind, head, h), out_rsem.at[kind, head, h]
            ).start()

        @pl.when(target != h)
        def _():
            pltpu.make_async_remote_copy(
                src_ref=out_src(kind, head, target),
                dst_ref=out_dst(kind, head, h),
                send_sem=out_ssem.at[kind, head, target],
                recv_sem=out_rsem.at[kind, head, h],
                device_id=(c, target),
                device_id_type=MESH,
            ).start()

    def give_back(side, slot):
        return pltpu.make_async_remote_copy(
            src_ref=ret_send.at[side, slot],
            dst_ref=ret_recv.at[side, slot],
            send_sem=ret_ssem.at[side, slot],
            recv_sem=ret_rsem.at[side, slot],
            device_id=(jnp.where(slot == 4, after, before), h),
            device_id_type=MESH,
        )

    for head in range(2):

        @pl.loop(0, n)
        def _(source):
            for kind in range(2):
                wait_in(2 + 2 * head + kind, source)

        @pl.loop(0, 4)
        def _(i):
            @pl.when(i < 3)
            def _():
                block(head, i, 5)

            @pl.when(i == 3)
            def _():
                block(head, i, 6)

            for kind in range(2):
                for part in range(2):
                    send_out(kind, head, 2 * i + part)
            if head == 1:
                ret_send[0, i] = dk_acc[i].astype(bf16)
                ret_send[1, i] = dv_acc[i].astype(bf16)
                for side in range(2):
                    give_back(side, i).start()

    ret_send[0, 4] = dk_acc[8].astype(bf16)
    ret_send[1, 4] = dv_acc[8].astype(bf16)
    for side in range(2):
        give_back(side, 4).start()

    def own_dst(side, source):
        return (gk_hbm, gv_hbm)[side].at[:, pl.ds(pl.multiple_of(source * HD, HD), HD)]

    def send_own(side, target):
        @pl.when(target == h)
        def _():
            pltpu.make_async_copy(
                own_buf.at[side, target], own_dst(side, h), own_rsem.at[side, h]
            ).start()

        @pl.when(target != h)
        def _():
            pltpu.make_async_remote_copy(
                src_ref=own_buf.at[side, target],
                dst_ref=own_dst(side, h),
                send_sem=own_ssem.at[side, target],
                recv_sem=own_rsem.at[side, h],
                device_id=(c, target),
                device_id_type=MESH,
            ).start()

    @pl.loop(0, 4)
    def _(tile):
        for side in range(2):
            give_back(side, tile).wait_recv()
            acc = (dk_acc, dv_acc)[side]

            @pl.when(tile == 0)
            def _():
                give_back(side, 4).wait_recv()
                acc[4] += ret_recv[side, 4].astype(f32)

            total = acc[4 + tile] + ret_recv[side, tile].astype(f32)
            own_buf[side, pl.ds(2 * tile, 2)] = total.astype(bf16).reshape(2, PIECE, HD)
            for part in range(2):
                send_own(side, 2 * tile + part)

    @pl.loop(0, n)
    def _(other):
        for kind in range(2):
            for head in range(2):
                dst = out_dst(kind, head, other)
                pltpu.make_async_copy(dst, dst, out_rsem.at[kind, head, other]).wait()
            dst = own_dst(kind, other)
            pltpu.make_async_copy(dst, dst, own_rsem.at[kind, other]).wait()
            forward(kind, other).wait_send()

        @pl.when(other != h)
        def _():
            for stream in range(6):
                src = in_src(stream, other)
                pltpu.make_async_copy(src, src, in_ssem.at[stream, other]).wait()
            for kind in range(2):
                for head in range(2):
                    src = out_src(kind, head, other)
                    pltpu.make_async_copy(src, src, out_ssem.at[kind, head, other]).wait()
                src = own_buf.at[kind, other]
                pltpu.make_async_copy(src, src, own_ssem.at[kind, other]).wait()

    @pl.loop(0, 5)
    def _(slot):
        for side in range(2):
            give_back(side, slot).wait_send()

    @pl.loop(0, 2)
    def _(piece):
        for side in range(2):
            ahead(side, piece).wait_send()


def local(queries, key_rows, value_rows, grad_out, doc_start, reach_end):
    dma = pltpu.SemaphoreType.DMA
    hbm = pl.BlockSpec(memory_space=pltpu.HBM)
    vmem = pl.BlockSpec(memory_space=pltpu.VMEM)
    return pl.pallas_call(
        kernel,
        out_shape=[
            jax.ShapeDtypeStruct(queries.shape, bf16),
            jax.ShapeDtypeStruct(queries.shape, bf16),
            jax.ShapeDtypeStruct(key_rows.shape, bf16),
            jax.ShapeDtypeStruct(key_rows.shape, bf16),
        ],
        in_specs=[hbm, hbm, hbm, hbm, vmem, vmem],
        out_specs=[hbm, hbm, hbm, hbm],
        scratch_shapes=[
            pltpu.VMEM((2, 8, PIECE, HD), bf16),
            pltpu.VMEM((2, 8, PIECE, HD), bf16),
            pltpu.VMEM((18, PIECE, HD), bf16),
            pltpu.VMEM((18, PIECE, HD), bf16),
            pltpu.VMEM((9, HD, TILE), bf16),
            pltpu.VMEM((9, HD, TILE), bf16),
            pltpu.VMEM((6, TILE, TILE), f32),
            pltpu.VMEM((9, TILE, HD), f32),
            pltpu.VMEM((9, TILE, HD), f32),
            pltpu.VMEM((2, 8, PIECE, HD), bf16),
            pltpu.VMEM((2, 8, PIECE, HD), bf16),
            pltpu.VMEM((2, 5, TILE, HD), bf16),
            pltpu.VMEM((2, 5, TILE, HD), bf16),
            pltpu.VMEM((2, 8, PIECE, HD), bf16),
            dma((6, 8)),
            dma((6, 8)),
            dma((2, 8)),
            dma((2, 8)),
            dma((2, 2)),
            dma((2, 2)),
            dma((2, 2, 8)),
            dma((2, 2, 8)),
            dma((2, 5)),
            dma((2, 5)),
            dma((2, 8)),
            dma((2, 8)),
        ],
        compiler_params=pltpu.CompilerParams(
            collective_id=0, has_side_effects=True, vmem_limit_bytes=40 * 1024 * 1024
        ),
    )(
        queries, key_rows, value_rows, grad_out,
        doc_start.reshape(4, 1, TILE), reach_end.reshape(4, 1, TILE),
    )


def solution(mesh):
    rows = P(("ctx", "head"), None)
    return jax.shard_map(
        local,
        mesh=mesh,
        in_specs=(rows, rows, rows, rows, P("ctx"), P("ctx")),
        out_specs=(rows, rows, rows, rows),
        check_vma=False,
    )
```

```python
import jax
import jax.numpy as jnp
from jax import lax
from jax.experimental import pallas as pl
from jax.experimental.pallas import tpu as pltpu
from jax.sharding import PartitionSpec as P

HD = 128
BLK = 1024
PIECE = 128
TILE = 256
WINDOW = 2304
SCALE = 168.0 ** (-0.5)
SCALE_LOG2 = SCALE * 1.4426950408889634
MASKED = -1e30
MESH = pl.DeviceIdType.MESH
f32 = jnp.float32
bf16 = jnp.bfloat16


def matmul(left, right):
    return lax.dot_general(left, right, (((1,), (0,)), ((), ())), preferred_element_type=f32)


def kernel(
    q_hbm, k_hbm, v_hbm, g_hbm, lower_hbm, upper_hbm,
    o_hbm, gq_hbm, gk_hbm, gv_hbm,
    lower_ref, upper_ref, q_buf, g_buf, k_win, v_win, kt_win, vt_win, s_buf, p_buf, ds_buf,
    gt_buf, gs_buf, qs_buf, delta_buf, scaled_buf, dk_acc, dv_acc,
    o_buf, gq_buf, ret_send, ret_recv, own_buf,
    mark_sem, in_ssem, in_rsem, fwd_ssem, fwd_rsem, ahead_ssem, ahead_rsem,
    out_ssem, out_rsem, ret_ssem, ret_rsem, own_ssem, own_rsem,
):
    n_ctx = lax.axis_size("ctx")
    n = lax.axis_size("head")
    c = lax.axis_index("ctx")
    h = lax.axis_index("head")
    after = lax.rem(c + 1, n_ctx)
    before = lax.rem(c + n_ctx - 1, n_ctx)

    barrier = pltpu.get_barrier_semaphore()

    @pl.loop(1, n)
    def _(r):
        pl.semaphore_signal(barrier, inc=1, device_id=(c, lax.rem(h + r, n)), device_id_type=MESH)

    pl.semaphore_signal(barrier, inc=1, device_id=(after, h), device_id_type=MESH)
    pl.semaphore_signal(barrier, inc=1, device_id=(before, h), device_id_type=MESH)
    pl.semaphore_wait(barrier, n + 1)

    def in_src(stream, target):
        if stream < 2:
            return (k_hbm, v_hbm)[stream].at[:, pl.ds(pl.multiple_of(target * HD, HD), HD)]
        head = (stream - 2) // 2
        cols = pl.ds(pl.multiple_of(target * 2 * HD + head * HD, HD), HD)
        return (q_hbm, g_hbm)[stream % 2].at[:, cols]

    def in_dst(stream, source):
        if stream < 2:
            return (k_win, v_win)[stream].at[8 + source]
        return (q_buf, g_buf)[stream % 2].at[(stream - 2) // 2, source]

    def send_in(streams):
        for stream in streams:
            pltpu.make_async_copy(
                in_src(stream, h), in_dst(stream, h), in_rsem.at[stream, h]
            ).start()

        @pl.loop(1, n)
        def _(r):
            target = lax.rem(h + r, n)
            for stream in streams:
                pltpu.make_async_remote_copy(
                    src_ref=in_src(stream, target),
                    dst_ref=in_dst(stream, h),
                    send_sem=in_ssem.at[stream, target],
                    recv_sem=in_rsem.at[stream, h],
                    device_id=(c, target),
                    device_id_type=MESH,
                ).start()

    def wait_in(stream, source):
        dst = in_dst(stream, source)
        pltpu.make_async_copy(dst, dst, in_rsem.at[stream, source]).wait()

    def forward(side, piece):
        win = (k_win, v_win)[side]
        return pltpu.make_async_remote_copy(
            src_ref=win.at[8 + piece],
            dst_ref=win.at[piece],
            send_sem=fwd_ssem.at[side, piece],
            recv_sem=fwd_rsem.at[side, piece],
            device_id=(after, h),
            device_id_type=MESH,
        )

    def ahead(side, piece):
        win = (k_win, v_win)[side]
        return pltpu.make_async_remote_copy(
            src_ref=win.at[8 + piece],
            dst_ref=win.at[16 + piece],
            send_sem=ahead_ssem.at[side, piece],
            recv_sem=ahead_rsem.at[side, piece],
            device_id=(before, h),
            device_id_type=MESH,
        )

    marks = [pltpu.make_async_copy(src, dst, mark_sem.at[k]) for k, (src, dst) in enumerate(
        ((lower_hbm, lower_ref), (upper_hbm, upper_ref)))]
    for mark in marks:
        mark.start()
    send_in((0, 1))
    send_in((2, 3))
    for piece in (7, 6, 0, 1, 5, 4, 3, 2):
        for side in range(2):
            wait_in(side, piece)
            if piece >= 2:
                forward(side, piece).start()
            else:
                ahead(side, piece).start()
    for piece in (1, 0):
        for side in range(2):
            forward(side, piece).start()
    send_in((4, 5))

    for mark in marks:
        mark.wait()
    dk_acc[...] = jnp.zeros_like(dk_acc)
    dv_acc[...] = jnp.zeros_like(dv_acc)

    def keys(tile):
        return k_win[2 * tile : 2 * tile + 2].reshape(TILE, HD)

    def values(tile):
        return v_win[2 * tile : 2 * tile + 2].reshape(TILE, HD)

    def turn(tile):
        rows = pl.ds(tile * TILE, TILE)
        kt_win[:, rows] = keys(tile).T
        vt_win[:, rows] = values(tile).T

    place = lax.broadcasted_iota(jnp.int32, (TILE, TILE), 0)

    def forward_block(head, i):
        tiles = 6 if i == 3 else 5
        rows = pl.ds(2 * i, 2)
        lanes = pl.ds(i * TILE, TILE)
        window = pl.ds(i * TILE, tiles * TILE)
        q = q_buf[head, rows].reshape(TILE, HD)
        g = g_buf[head, rows].reshape(TILE, HD)
        qt = q.T
        gt = g.T
        gt_buf[:, lanes] = gt
        first = (c - 1) * BLK + i * TILE
        lower = lower_ref[i] - first
        upper = upper_ref[i] - first
        top = None
        for t in range(tiles):
            s = matmul(keys(i + t), qt) * SCALE_LOG2
            allowed = place >= lower - t * TILE
            if t >= 4:
                allowed = allowed & (place <= upper - t * TILE)
            s = jnp.where(allowed, s, MASKED)
            s_buf[t] = s
            most = jnp.max(s, axis=0, keepdims=True)
            top = most if top is None else jnp.maximum(top, most)
        total = None
        for t in range(tiles):
            p = jnp.exp2(s_buf[t] - top)
            p_buf[pl.ds((i + t) * TILE, TILE), lanes] = p.astype(bf16)
            part = jnp.sum(p, axis=0, keepdims=True)
            total = part if total is None else total + part
        share = 1.0 / total
        out = (matmul(vt_win[:, window], p_buf[window, lanes]) * share).astype(bf16)
        o_buf[head, rows] = out.T.reshape(2, PIECE, HD)
        gt = gt.astype(f32)
        delta_buf[i] = jnp.sum(gt * out.astype(f32), axis=0, keepdims=True)
        scaled = share * SCALE
        scaled_buf[i] = scaled
        gs_buf[lanes] = (gt * share).astype(bf16).T
        qs_buf[lanes] = (qt.astype(f32) * scaled).astype(bf16).T

    def backward_tile(tile):
        blocks = range(max(0, tile - 4), 1 + min(3, tile)) if tile < 8 else range(3, 4)
        rows = pl.ds(tile * TILE, TILE)
        span = pl.ds(blocks[0] * TILE, len(blocks) * TILE)
        v = values(tile)
        dv_acc[tile] += matmul(p_buf[rows, span], gs_buf[span])
        for i in blocks:
            lanes = pl.ds(i * TILE, TILE)
            dp = matmul(v, gt_buf[:, lanes])
            ds_buf[rows, lanes] = p_buf[rows, lanes] * (dp - delta_buf[i]).astype(bf16)
        dk_acc[tile] += matmul(ds_buf[rows, span], qs_buf[span])

    def grad_queries(head, i):
        lanes = pl.ds(i * TILE, TILE)
        window = pl.ds(i * TILE, (6 if i == 3 else 5) * TILE)
        grad = matmul(kt_win[:, window], ds_buf[window, lanes]) * scaled_buf[i]
        gq_buf[head, pl.ds(2 * i, 2)] = grad.astype(bf16).T.reshape(2, PIECE, HD)

    def out_src(kind, head, target):
        return (o_buf, gq_buf)[kind].at[head, target]

    def out_dst(kind, head, source):
        cols = pl.ds(pl.multiple_of(source * 2 * HD + head * HD, HD), HD)
        return (o_hbm, gq_hbm)[kind].at[:, cols]

    def send_out(kind, head, target):
        @pl.when(target == h)
        def _():
            pltpu.make_async_copy(
                out_src(kind, head, target), out_dst(kind, head, h), out_rsem.at[kind, head, h]
            ).start()

        @pl.when(target != h)
        def _():
            pltpu.make_async_remote_copy(
                src_ref=out_src(kind, head, target),
                dst_ref=out_dst(kind, head, h),
                send_sem=out_ssem.at[kind, head, target],
                recv_sem=out_rsem.at[kind, head, h],
                device_id=(c, target),
                device_id_type=MESH,
            ).start()

    def give_back(side, slot):
        return pltpu.make_async_remote_copy(
            src_ref=ret_send.at[side, slot],
            dst_ref=ret_recv.at[side, slot],
            send_sem=ret_ssem.at[side, slot],
            recv_sem=ret_rsem.at[side, slot],
            device_id=(jnp.where(slot == 4, after, before), h),
            device_id_type=MESH,
        )

    def own_dst(side, source):
        return (gk_hbm, gv_hbm)[side].at[:, pl.ds(pl.multiple_of(source * HD, HD), HD)]

    def send_own(side, target):
        @pl.when(target == h)
        def _():
            pltpu.make_async_copy(
                own_buf.at[side, target], own_dst(side, h), own_rsem.at[side, h]
            ).start()

        @pl.when(target != h)
        def _():
            pltpu.make_async_remote_copy(
                src_ref=own_buf.at[side, target],
                dst_ref=own_dst(side, h),
                send_sem=own_ssem.at[side, target],
                recv_sem=own_rsem.at[side, h],
                device_id=(c, target),
                device_id_type=MESH,
            ).start()

    def send_sum(tile):
        for side in range(2):
            give_back(side, tile).wait_recv()
            acc = (dk_acc, dv_acc)[side]
            total = acc[4 + tile] + ret_recv[side, tile].astype(f32)
            if tile == 0:
                give_back(side, 4).wait_recv()
                total += ret_recv[side, 4].astype(f32)
            own_buf[side, 2 * tile : 2 * tile + 2] = total.astype(bf16).reshape(2, PIECE, HD)
            for part in range(2):
                send_own(side, 2 * tile + part)

    def send_back(slot):
        tile = 8 if slot == 4 else slot
        for side in range(2):
            ret_send[side, slot] = (dk_acc, dv_acc)[side][tile].astype(bf16)
            give_back(side, slot).start()

    @pl.loop(0, 2)
    def _(head):
        @pl.loop(0, n)
        def _(source):
            for kind in range(2):
                dst = (q_buf, g_buf)[kind].at[head, source]
                pltpu.make_async_copy(dst, dst, in_rsem.at[2 + 2 * head + kind, source]).wait()

        for i in (3, 2, 1, 0):
            @pl.when(head == 0)
            def _():
                for piece in (2 * i, 2 * i + 1):
                    for side in range(2):
                        forward(side, piece).wait_recv()
                turn(i)
                if i == 3:
                    for piece in range(2):
                        for side in range(2):
                            ahead(side, piece).wait_recv()
                    for tile in range(4, 9):
                        turn(tile)

            forward_block(head, i)
            for part in range(2):
                send_out(0, head, 2 * i + part)

        for tile in (0, 1, 2, 3, 8, 4, 5, 6, 7):
            backward_tile(tile)
            if tile in (0, 1, 2, 3, 8):
                @pl.when(head == 1)
                def _():
                    send_back(min(tile, 4))
            else:
                grad_queries(head, tile - 4)
                for part in range(2):
                    send_out(1, head, 2 * (tile - 4) + part)
            if tile in (6, 7):
                @pl.when(head == 1)
                def _():
                    for own in ((0, 1) if tile == 6 else (2, 3)):
                        send_sum(own)

    @pl.loop(0, n)
    def _(other):
        for kind in range(2):
            for head in range(2):
                dst = out_dst(kind, head, other)
                pltpu.make_async_copy(dst, dst, out_rsem.at[kind, head, other]).wait()
            dst = own_dst(kind, other)
            pltpu.make_async_copy(dst, dst, own_rsem.at[kind, other]).wait()
            forward(kind, other).wait_send()

        @pl.when(other != h)
        def _():
            for stream in range(6):
                src = in_src(stream, other)
                pltpu.make_async_copy(src, src, in_ssem.at[stream, other]).wait()
            for kind in range(2):
                for head in range(2):
                    src = out_src(kind, head, other)
                    pltpu.make_async_copy(src, src, out_ssem.at[kind, head, other]).wait()
                src = own_buf.at[kind, other]
                pltpu.make_async_copy(src, src, own_ssem.at[kind, other]).wait()

    @pl.loop(0, 5)
    def _(slot):
        for side in range(2):
            give_back(side, slot).wait_send()

    @pl.loop(0, 2)
    def _(piece):
        for side in range(2):
            ahead(side, piece).wait_send()


def place_results(*refs):
    copies = [pltpu.make_async_copy(refs[k], refs[4 + k], refs[8].at[k]) for k in range(4)]
    for copy in copies:
        copy.start()
    for copy in copies:
        copy.wait()


def local(queries, key_rows, value_rows, grad_out, doc_start, reach_end):
    dma = pltpu.SemaphoreType.DMA
    hbm = pl.BlockSpec(memory_space=pltpu.HBM)
    results = pl.pallas_call(
        kernel,
        out_shape=[
            jax.ShapeDtypeStruct(queries.shape, bf16),
            jax.ShapeDtypeStruct(queries.shape, bf16),
            jax.ShapeDtypeStruct(key_rows.shape, bf16),
            jax.ShapeDtypeStruct(key_rows.shape, bf16),
        ],
        in_specs=[hbm] * 6,
        out_specs=[hbm, hbm, hbm, hbm],
        scratch_shapes=[
            pltpu.VMEM((4, 1, TILE), jnp.int32),
            pltpu.VMEM((4, 1, TILE), jnp.int32),
            pltpu.VMEM((2, 8, PIECE, HD), bf16),
            pltpu.VMEM((2, 8, PIECE, HD), bf16),
            pltpu.VMEM((18, PIECE, HD), bf16),
            pltpu.VMEM((18, PIECE, HD), bf16),
            pltpu.VMEM((HD, WINDOW), bf16),
            pltpu.VMEM((HD, WINDOW), bf16),
            pltpu.VMEM((6, TILE, TILE), f32),
            pltpu.VMEM((WINDOW, BLK), bf16),
            pltpu.VMEM((WINDOW, BLK), bf16),
            pltpu.VMEM((HD, BLK), bf16),
            pltpu.VMEM((BLK, HD), bf16),
            pltpu.VMEM((BLK, HD), bf16),
            pltpu.VMEM((4, 1, TILE), f32),
            pltpu.VMEM((4, 1, TILE), f32),
            pltpu.VMEM((9, TILE, HD), f32),
            pltpu.VMEM((9, TILE, HD), f32),
            pltpu.VMEM((2, 8, PIECE, HD), bf16),
            pltpu.VMEM((2, 8, PIECE, HD), bf16),
            pltpu.VMEM((2, 5, TILE, HD), bf16),
            pltpu.VMEM((2, 5, TILE, HD), bf16),
            pltpu.VMEM((2, 8, PIECE, HD), bf16),
            dma((2,)),
            dma((6, 8)),
            dma((6, 8)),
            dma((2, 8)),
            dma((2, 8)),
            dma((2, 2)),
            dma((2, 2)),
            dma((2, 2, 8)),
            dma((2, 2, 8)),
            dma((2, 5)),
            dma((2, 5)),
            dma((2, 8)),
            dma((2, 8)),
        ],
        compiler_params=pltpu.CompilerParams(
            collective_id=0, has_side_effects=True, vmem_limit_bytes=63 * 1024 * 1024
        ),
    )(
        queries, key_rows, value_rows, grad_out,
        doc_start.reshape(4, 1, TILE), reach_end.reshape(4, 1, TILE),
    )
    return pl.pallas_call(
        place_results,
        out_shape=[jax.ShapeDtypeStruct(r.shape, r.dtype) for r in results],
        in_specs=[hbm] * 4,
        out_specs=[hbm] * 4,
        scratch_shapes=[dma((4,))],
        compiler_params=pltpu.CompilerParams(vmem_limit_bytes=63 * 1024 * 1024),
    )(*results)


def solution(mesh):
    rows = P(("ctx", "head"), None)
    return jax.shard_map(
        local,
        mesh=mesh,
        in_specs=(rows, rows, rows, rows, P("ctx"), P("ctx")),
        out_specs=(rows, rows, rows, rows),
        check_vma=False,
    )
```

```python
import jax
import jax.numpy as jnp
from jax import lax
from jax.experimental import pallas as pl
from jax.experimental.pallas import tpu as pltpu
from jax.sharding import PartitionSpec as P

HD = 128
BLK = 1024
PIECE = 128
TILE = 256
WINDOW = 2304
SCALE = 168.0 ** (-0.5)
SCALE_LOG2 = SCALE * 1.4426950408889634
MASKED = -1e30
MESH = pl.DeviceIdType.MESH
f32 = jnp.float32
bf16 = jnp.bfloat16


def matmul(left, right):
    return lax.dot_general(left, right, (((1,), (0,)), ((), ())), preferred_element_type=f32)


def kernel(
    q_hbm, k_hbm, v_hbm, g_hbm, lower_hbm, upper_hbm,
    o_hbm, gq_hbm, gk_hbm, gv_hbm,
    lower_ref, upper_ref, q_buf, g_buf, k_win, v_win, kt_win, vt_win, s_buf, p_buf, ds_buf,
    gt_buf, gs_buf, qs_buf, delta_buf, scaled_buf, dk_acc, dv_acc,
    o_buf, gq_buf, ret_send, ret_recv, own_buf,
    q_own, k_own, v_own, g_own, stage_sem, mark_sem, in_ssem, in_rsem, fwd_ssem, fwd_rsem, ahead_ssem, ahead_rsem,
    out_ssem, out_rsem, ret_ssem, ret_rsem, own_ssem, own_rsem,
):
    n_ctx = lax.axis_size("ctx")
    n = lax.axis_size("head")
    c = lax.axis_index("ctx")
    h = lax.axis_index("head")
    after = lax.rem(c + 1, n_ctx)
    before = lax.rem(c + n_ctx - 1, n_ctx)

    stages = [
        pltpu.make_async_copy(src, dst, stage_sem.at[k])
        for k, (src, dst) in enumerate(
            ((k_hbm, k_own), (v_hbm, v_own), (q_hbm, q_own), (g_hbm, g_own))
        )
    ]
    for stage in stages:
        stage.start()

    barrier = pltpu.get_barrier_semaphore()

    @pl.loop(1, n)
    def _(r):
        pl.semaphore_signal(barrier, inc=1, device_id=(c, lax.rem(h + r, n)), device_id_type=MESH)

    pl.semaphore_signal(barrier, inc=1, device_id=(after, h), device_id_type=MESH)
    pl.semaphore_signal(barrier, inc=1, device_id=(before, h), device_id_type=MESH)
    pl.semaphore_wait(barrier, n + 1)

    def in_src(stream, target):
        if stream < 2:
            return (k_own, v_own)[stream].at[:, pl.ds(pl.multiple_of(target * HD, HD), HD)]
        head = (stream - 2) // 2
        cols = pl.ds(pl.multiple_of(target * 2 * HD + head * HD, HD), HD)
        return (q_own, g_own)[stream % 2].at[:, cols]

    def in_dst(stream, source):
        if stream < 2:
            return (k_win, v_win)[stream].at[8 + source]
        return (q_buf, g_buf)[stream % 2].at[(stream - 2) // 2, source]

    def send_in(streams):
        for stream in streams:
            pltpu.make_async_copy(
                in_src(stream, h), in_dst(stream, h), in_rsem.at[stream, h]
            ).start()

        @pl.loop(1, n)
        def _(r):
            target = lax.rem(h + r, n)
            for stream in streams:
                pltpu.make_async_remote_copy(
                    src_ref=in_src(stream, target),
                    dst_ref=in_dst(stream, h),
                    send_sem=in_ssem.at[stream, target],
                    recv_sem=in_rsem.at[stream, h],
                    device_id=(c, target),
                    device_id_type=MESH,
                ).start()

    def wait_in(stream, source):
        dst = in_dst(stream, source)
        pltpu.make_async_copy(dst, dst, in_rsem.at[stream, source]).wait()

    def forward(side, piece):
        win = (k_win, v_win)[side]
        return pltpu.make_async_remote_copy(
            src_ref=win.at[8 + piece],
            dst_ref=win.at[piece],
            send_sem=fwd_ssem.at[side, piece],
            recv_sem=fwd_rsem.at[side, piece],
            device_id=(after, h),
            device_id_type=MESH,
        )

    def ahead(side, piece):
        win = (k_win, v_win)[side]
        return pltpu.make_async_remote_copy(
            src_ref=win.at[8 + piece],
            dst_ref=win.at[16 + piece],
            send_sem=ahead_ssem.at[side, piece],
            recv_sem=ahead_rsem.at[side, piece],
            device_id=(before, h),
            device_id_type=MESH,
        )

    marks = [
        pltpu.make_async_copy(src, dst, mark_sem.at[k])
        for k, (src, dst) in enumerate(((lower_hbm, lower_ref), (upper_hbm, upper_ref)))
    ]
    for mark in marks:
        mark.start()
    stages[0].wait()
    stages[1].wait()
    send_in((0, 1))
    stages[2].wait()
    stages[3].wait()
    send_in((2, 3))
    for piece in (7, 6, 0, 1, 5, 4, 3, 2):
        for side in range(2):
            wait_in(side, piece)
            if piece >= 2:
                forward(side, piece).start()
            else:
                ahead(side, piece).start()
    for piece in (1, 0):
        for side in range(2):
            forward(side, piece).start()
    send_in((4, 5))

    for mark in marks:
        mark.wait()
    dk_acc[...] = jnp.zeros_like(dk_acc)
    dv_acc[...] = jnp.zeros_like(dv_acc)

    def keys(tile):
        return k_win[2 * tile : 2 * tile + 2].reshape(TILE, HD)

    def values(tile):
        return v_win[2 * tile : 2 * tile + 2].reshape(TILE, HD)

    def turn(tile):
        rows = pl.ds(tile * TILE, TILE)
        kt_win[:, rows] = keys(tile).T
        vt_win[:, rows] = values(tile).T

    place = lax.broadcasted_iota(jnp.int32, (TILE, TILE), 0)

    def forward_block(head, i):
        tiles = 6 if i == 3 else 5
        rows = pl.ds(2 * i, 2)
        lanes = pl.ds(i * TILE, TILE)
        window = pl.ds(i * TILE, tiles * TILE)
        q = q_buf[head, rows].reshape(TILE, HD)
        g = g_buf[head, rows].reshape(TILE, HD)
        qt = q.T
        gt = g.T
        gt_buf[:, lanes] = gt
        first = (c - 1) * BLK + i * TILE
        lower = lower_ref[i] - first
        upper = upper_ref[i] - first
        top = None
        for t in range(tiles):
            s = matmul(keys(i + t), qt) * SCALE_LOG2
            allowed = place >= lower - t * TILE
            if t >= 4:
                allowed = allowed & (place <= upper - t * TILE)
            s = jnp.where(allowed, s, MASKED)
            s_buf[t] = s
            most = jnp.max(s, axis=0, keepdims=True)
            top = most if top is None else jnp.maximum(top, most)
        total = None
        for t in range(tiles):
            p = jnp.exp2(s_buf[t] - top)
            p_buf[pl.ds((i + t) * TILE, TILE), lanes] = p.astype(bf16)
            part = jnp.sum(p, axis=0, keepdims=True)
            total = part if total is None else total + part
        share = 1.0 / total
        out = (matmul(vt_win[:, window], p_buf[window, lanes]) * share).astype(bf16)
        o_buf[head, rows] = out.T.reshape(2, PIECE, HD)
        gt = gt.astype(f32)
        delta_buf[i] = jnp.sum(gt * out.astype(f32), axis=0, keepdims=True)
        scaled = share * SCALE
        scaled_buf[i] = scaled
        gs_buf[lanes] = (gt * share).astype(bf16).T
        qs_buf[lanes] = (qt.astype(f32) * scaled).astype(bf16).T

    def backward_tile(tile):
        blocks = range(max(0, tile - 4), 1 + min(3, tile)) if tile < 8 else range(3, 4)
        rows = pl.ds(tile * TILE, TILE)
        span = pl.ds(blocks[0] * TILE, len(blocks) * TILE)
        v = values(tile)
        dv_acc[tile] += matmul(p_buf[rows, span], gs_buf[span])
        for i in blocks:
            lanes = pl.ds(i * TILE, TILE)
            dp = matmul(v, gt_buf[:, lanes])
            ds_buf[rows, lanes] = p_buf[rows, lanes] * (dp - delta_buf[i]).astype(bf16)
        dk_acc[tile] += matmul(ds_buf[rows, span], qs_buf[span])

    def grad_queries(head, i):
        lanes = pl.ds(i * TILE, TILE)
        window = pl.ds(i * TILE, (6 if i == 3 else 5) * TILE)
        grad = matmul(kt_win[:, window], ds_buf[window, lanes]) * scaled_buf[i]
        gq_buf[head, pl.ds(2 * i, 2)] = grad.astype(bf16).T.reshape(2, PIECE, HD)

    def out_src(kind, head, target):
        return (o_buf, gq_buf)[kind].at[head, target]

    def out_dst(kind, head, source):
        cols = pl.ds(pl.multiple_of(source * 2 * HD + head * HD, HD), HD)
        return (o_hbm, gq_hbm)[kind].at[:, cols]

    def send_out(kind, head, target):
        @pl.when(target == h)
        def _():
            pltpu.make_async_copy(
                out_src(kind, head, target), out_dst(kind, head, h), out_rsem.at[kind, head, h]
            ).start()

        @pl.when(target != h)
        def _():
            pltpu.make_async_remote_copy(
                src_ref=out_src(kind, head, target),
                dst_ref=out_dst(kind, head, h),
                send_sem=out_ssem.at[kind, head, target],
                recv_sem=out_rsem.at[kind, head, h],
                device_id=(c, target),
                device_id_type=MESH,
            ).start()

    def give_back(side, slot):
        return pltpu.make_async_remote_copy(
            src_ref=ret_send.at[side, slot],
            dst_ref=ret_recv.at[side, slot],
            send_sem=ret_ssem.at[side, slot],
            recv_sem=ret_rsem.at[side, slot],
            device_id=(jnp.where(slot == 4, after, before), h),
            device_id_type=MESH,
        )

    def own_dst(side, source):
        return (gk_hbm, gv_hbm)[side].at[:, pl.ds(pl.multiple_of(source * HD, HD), HD)]

    def send_own(side, target):
        @pl.when(target == h)
        def _():
            pltpu.make_async_copy(
                own_buf.at[side, target], own_dst(side, h), own_rsem.at[side, h]
            ).start()

        @pl.when(target != h)
        def _():
            pltpu.make_async_remote_copy(
                src_ref=own_buf.at[side, target],
                dst_ref=own_dst(side, h),
                send_sem=own_ssem.at[side, target],
                recv_sem=own_rsem.at[side, h],
                device_id=(c, target),
                device_id_type=MESH,
            ).start()

    def send_sum(tile):
        for side in range(2):
            give_back(side, tile).wait_recv()
            acc = (dk_acc, dv_acc)[side]
            total = acc[4 + tile] + ret_recv[side, tile].astype(f32)
            if tile == 0:
                give_back(side, 4).wait_recv()
                total += ret_recv[side, 4].astype(f32)
            own_buf[side, 2 * tile : 2 * tile + 2] = total.astype(bf16).reshape(2, PIECE, HD)
            for part in range(2):
                send_own(side, 2 * tile + part)

    def send_back(slot):
        tile = 8 if slot == 4 else slot
        for side in range(2):
            ret_send[side, slot] = (dk_acc, dv_acc)[side][tile].astype(bf16)
            give_back(side, slot).start()

    @pl.loop(0, 2)
    def _(head):
        @pl.loop(0, n)
        def _(source):
            for kind in range(2):
                dst = (q_buf, g_buf)[kind].at[head, source]
                pltpu.make_async_copy(dst, dst, in_rsem.at[2 + 2 * head + kind, source]).wait()

        for i in (3, 2, 1, 0):
            @pl.when(head == 0)
            def _():
                for piece in (2 * i, 2 * i + 1):
                    for side in range(2):
                        forward(side, piece).wait_recv()
                turn(i)
                if i == 3:
                    for piece in range(2):
                        for side in range(2):
                            ahead(side, piece).wait_recv()
                    for tile in range(4, 9):
                        turn(tile)

            forward_block(head, i)
            for part in range(2):
                send_out(0, head, 2 * i + part)

        for tile in (0, 1, 2, 3, 8, 4, 5, 6, 7):
            backward_tile(tile)
            if tile in (0, 1, 2, 3, 8):
                @pl.when(head == 1)
                def _():
                    send_back(min(tile, 4))
            else:
                grad_queries(head, tile - 4)
                for part in range(2):
                    send_out(1, head, 2 * (tile - 4) + part)
            if tile in (6, 7):
                @pl.when(head == 1)
                def _():
                    for own in ((0, 1) if tile == 6 else (2, 3)):
                        send_sum(own)

    @pl.loop(0, n)
    def _(other):
        for kind in range(2):
            for head in range(2):
                dst = out_dst(kind, head, other)
                pltpu.make_async_copy(dst, dst, out_rsem.at[kind, head, other]).wait()
            dst = own_dst(kind, other)
            pltpu.make_async_copy(dst, dst, own_rsem.at[kind, other]).wait()
            forward(kind, other).wait_send()

        @pl.when(other != h)
        def _():
            for stream in range(6):
                src = in_src(stream, other)
                pltpu.make_async_copy(src, src, in_ssem.at[stream, other]).wait()
            for kind in range(2):
                for head in range(2):
                    src = out_src(kind, head, other)
                    pltpu.make_async_copy(src, src, out_ssem.at[kind, head, other]).wait()
                src = own_buf.at[kind, other]
                pltpu.make_async_copy(src, src, own_ssem.at[kind, other]).wait()

    @pl.loop(0, 5)
    def _(slot):
        for side in range(2):
            give_back(side, slot).wait_send()

    @pl.loop(0, 2)
    def _(piece):
        for side in range(2):
            ahead(side, piece).wait_send()


def place_results(*refs):
    sources, places, held, sems = refs[:4], refs[4:8], refs[8:12], refs[12]
    reads = [pltpu.make_async_copy(sources[k], held[k], sems.at[0, k]) for k in range(4)]
    writes = [pltpu.make_async_copy(held[k], places[k], sems.at[1, k]) for k in range(4)]
    for read in reads:
        read.start()
    for read, write in zip(reads, writes):
        read.wait()
        write.start()
    for write in writes:
        write.wait()


def local(queries, key_rows, value_rows, grad_out, doc_start, reach_end):
    dma = pltpu.SemaphoreType.DMA
    hbm = pl.BlockSpec(memory_space=pltpu.HBM)
    results = pl.pallas_call(
        kernel,
        out_shape=[
            jax.ShapeDtypeStruct(queries.shape, bf16),
            jax.ShapeDtypeStruct(queries.shape, bf16),
            jax.ShapeDtypeStruct(key_rows.shape, bf16),
            jax.ShapeDtypeStruct(key_rows.shape, bf16),
        ],
        in_specs=[hbm] * 6,
        out_specs=[hbm, hbm, hbm, hbm],
        scratch_shapes=[
            pltpu.VMEM((4, 1, TILE), jnp.int32),
            pltpu.VMEM((4, 1, TILE), jnp.int32),
            pltpu.VMEM((2, 8, PIECE, HD), bf16),
            pltpu.VMEM((2, 8, PIECE, HD), bf16),
            pltpu.VMEM((18, PIECE, HD), bf16),
            pltpu.VMEM((18, PIECE, HD), bf16),
            pltpu.VMEM((HD, WINDOW), bf16),
            pltpu.VMEM((HD, WINDOW), bf16),
            pltpu.VMEM((6, TILE, TILE), f32),
            pltpu.VMEM((WINDOW, BLK), bf16),
            pltpu.VMEM((WINDOW, BLK), bf16),
            pltpu.VMEM((HD, BLK), bf16),
            pltpu.VMEM((BLK, HD), bf16),
            pltpu.VMEM((BLK, HD), bf16),
            pltpu.VMEM((4, 1, TILE), f32),
            pltpu.VMEM((4, 1, TILE), f32),
            pltpu.VMEM((9, TILE, HD), f32),
            pltpu.VMEM((9, TILE, HD), f32),
            pltpu.VMEM((2, 8, PIECE, HD), bf16),
            pltpu.VMEM((2, 8, PIECE, HD), bf16),
            pltpu.VMEM((2, 5, TILE, HD), bf16),
            pltpu.VMEM((2, 5, TILE, HD), bf16),
            pltpu.VMEM((2, 8, PIECE, HD), bf16),
            pltpu.VMEM((PIECE, 16 * HD), bf16),
            pltpu.VMEM((PIECE, 8 * HD), bf16),
            pltpu.VMEM((PIECE, 8 * HD), bf16),
            pltpu.VMEM((PIECE, 16 * HD), bf16),
            dma((4,)),
            dma((2,)),
            dma((6, 8)),
            dma((6, 8)),
            dma((2, 8)),
            dma((2, 8)),
            dma((2, 2)),
            dma((2, 2)),
            dma((2, 2, 8)),
            dma((2, 2, 8)),
            dma((2, 5)),
            dma((2, 5)),
            dma((2, 8)),
            dma((2, 8)),
        ],
        compiler_params=pltpu.CompilerParams(
            collective_id=0, has_side_effects=True, vmem_limit_bytes=63 * 1024 * 1024
        ),
    )(
        queries, key_rows, value_rows, grad_out,
        doc_start.reshape(4, 1, TILE), reach_end.reshape(4, 1, TILE),
    )
    return pl.pallas_call(
        place_results,
        out_shape=[jax.ShapeDtypeStruct(r.shape, r.dtype) for r in results],
        in_specs=[hbm] * 4,
        out_specs=[hbm] * 4,
        scratch_shapes=[pltpu.VMEM(r.shape, r.dtype) for r in results] + [dma((2, 4))],
        compiler_params=pltpu.CompilerParams(vmem_limit_bytes=63 * 1024 * 1024),
    )(*results)


def solution(mesh):
    rows = P(("ctx", "head"), None)
    return jax.shard_map(
        local,
        mesh=mesh,
        in_specs=(rows, rows, rows, rows, P("ctx"), P("ctx")),
        out_specs=(rows, rows, rows, rows),
        check_vma=False,
    )
```

```python
import jax
import jax.numpy as jnp
from jax import lax
from jax.experimental import pallas as pl
from jax.experimental.pallas import tpu as pltpu
from jax.sharding import PartitionSpec as P

HD = 128
BLK = 1024
PIECE = 128
TILE = 256
WINDOW = 2304
SCALE = 168.0 ** (-0.5)
SCALE_LOG2 = SCALE * 1.4426950408889634
MASKED = -1e30
MESH = pl.DeviceIdType.MESH
f32 = jnp.float32
bf16 = jnp.bfloat16


def matmul(left, right):
    return lax.dot_general(left, right, (((1,), (0,)), ((), ())), preferred_element_type=f32)


def kernel(
    q_hbm, k_hbm, v_hbm, g_hbm, lower_hbm, upper_hbm,
    o_hbm, gq_hbm, gk_hbm, gv_hbm,
    lower_ref, upper_ref, q_buf, g_buf, k_win, v_win, kt_win, vt_win, s_buf, p_buf, ds_buf,
    gt_buf, gs_buf, qs_buf, delta_buf, scaled_buf, dk_acc, dv_acc,
    o_buf, gq_buf, ret_send, ret_recv, own_buf,
    q_own, k_own, v_own, g_own, stage_sem, mark_sem, in_ssem, in_rsem, fwd_ssem, fwd_rsem, ahead_ssem, ahead_rsem,
    out_ssem, out_rsem, ret_ssem, ret_rsem, own_ssem, own_rsem,
):
    n_ctx = lax.axis_size("ctx")
    n = lax.axis_size("head")
    c = lax.axis_index("ctx")
    h = lax.axis_index("head")
    after = lax.rem(c + 1, n_ctx)
    before = lax.rem(c + n_ctx - 1, n_ctx)
    has_after = c < n_ctx - 1
    has_before = c > 0

    stages = [
        pltpu.make_async_copy(src, dst, stage_sem.at[k])
        for k, (src, dst) in enumerate(
            ((k_hbm, k_own), (v_hbm, v_own), (q_hbm, q_own), (g_hbm, g_own))
        )
    ]
    for stage in stages:
        stage.start()

    barrier = pltpu.get_barrier_semaphore()

    @pl.loop(1, n)
    def _(r):
        pl.semaphore_signal(barrier, inc=1, device_id=(c, lax.rem(h + r, n)), device_id_type=MESH)

    @pl.when(has_after)
    def _():
        pl.semaphore_signal(barrier, inc=1, device_id=(after, h), device_id_type=MESH)

    @pl.when(has_before)
    def _():
        pl.semaphore_signal(barrier, inc=1, device_id=(before, h), device_id_type=MESH)

    neighbours = jnp.where(has_after, 1, 0) + jnp.where(has_before, 1, 0)
    pl.semaphore_wait(barrier, n - 1 + neighbours)

    def in_src(stream, target):
        if stream < 2:
            return (k_own, v_own)[stream].at[:, pl.ds(pl.multiple_of(target * HD, HD), HD)]
        head = (stream - 2) // 2
        cols = pl.ds(pl.multiple_of(target * 2 * HD + head * HD, HD), HD)
        return (q_own, g_own)[stream % 2].at[:, cols]

    def in_dst(stream, source):
        if stream < 2:
            return (k_win, v_win)[stream].at[8 + source]
        return (q_buf, g_buf)[stream % 2].at[(stream - 2) // 2, source]

    def send_in(streams):
        for stream in streams:
            pltpu.make_async_copy(
                in_src(stream, h), in_dst(stream, h), in_rsem.at[stream, h]
            ).start()

        @pl.loop(1, n)
        def _(r):
            target = lax.rem(h + r, n)
            for stream in streams:
                pltpu.make_async_remote_copy(
                    src_ref=in_src(stream, target),
                    dst_ref=in_dst(stream, h),
                    send_sem=in_ssem.at[stream, target],
                    recv_sem=in_rsem.at[stream, h],
                    device_id=(c, target),
                    device_id_type=MESH,
                ).start()

    def wait_in(stream, source):
        dst = in_dst(stream, source)
        pltpu.make_async_copy(dst, dst, in_rsem.at[stream, source]).wait()

    def forward(side, piece):
        win = (k_win, v_win)[side]
        return pltpu.make_async_remote_copy(
            src_ref=win.at[8 + piece],
            dst_ref=win.at[piece],
            send_sem=fwd_ssem.at[side, piece],
            recv_sem=fwd_rsem.at[side, piece],
            device_id=(after, h),
            device_id_type=MESH,
        )

    def ahead(side, piece):
        win = (k_win, v_win)[side]
        return pltpu.make_async_remote_copy(
            src_ref=win.at[8 + piece],
            dst_ref=win.at[16 + piece],
            send_sem=ahead_ssem.at[side, piece],
            recv_sem=ahead_rsem.at[side, piece],
            device_id=(before, h),
            device_id_type=MESH,
        )

    marks = [
        pltpu.make_async_copy(src, dst, mark_sem.at[k])
        for k, (src, dst) in enumerate(((lower_hbm, lower_ref), (upper_hbm, upper_ref)))
    ]
    for mark in marks:
        mark.start()
    stages[0].wait()
    stages[1].wait()
    send_in((0, 1))
    stages[2].wait()
    stages[3].wait()
    send_in((2, 3))
    for piece in (7, 6, 0, 1, 5, 4, 3, 2):
        for side in range(2):
            wait_in(side, piece)
            if piece >= 2:
                pl.when(has_after)(forward(side, piece).start)
            else:
                pl.when(has_before)(ahead(side, piece).start)

    @pl.when(has_after)
    def _():
        for piece in (1, 0):
            for side in range(2):
                forward(side, piece).start()

    send_in((4, 5))

    @pl.when(jnp.logical_not(has_before))
    def _():
        for side in range(2):
            (k_win, v_win)[side][0:8] = jnp.zeros((8, PIECE, HD), bf16)
            ret_recv[side, 4] = jnp.zeros((TILE, HD), bf16)

    @pl.when(jnp.logical_not(has_after))
    def _():
        for side in range(2):
            (k_win, v_win)[side][16:18] = jnp.zeros((2, PIECE, HD), bf16)
            ret_recv[side, 0:4] = jnp.zeros((4, TILE, HD), bf16)

    for mark in marks:
        mark.wait()
    def keys(tile):
        return k_win[2 * tile : 2 * tile + 2].reshape(TILE, HD)

    def values(tile):
        return v_win[2 * tile : 2 * tile + 2].reshape(TILE, HD)

    def turn(tile):
        rows = pl.ds(tile * TILE, TILE)
        kt_win[:, rows] = keys(tile).T
        vt_win[:, rows] = values(tile).T

    for tile in range(4, 8):
        turn(tile)
    dk_acc[...] = jnp.zeros_like(dk_acc)
    dv_acc[...] = jnp.zeros_like(dv_acc)
    place = lax.broadcasted_iota(jnp.int32, (TILE, TILE), 0)

    def scores(head, i):
        rows = pl.ds(2 * i, 2)
        qt = q_buf[head, rows].reshape(TILE, HD).T
        gt_buf[:, pl.ds(i * TILE, TILE)] = g_buf[head, rows].reshape(TILE, HD).T
        first = (c - 1) * BLK + i * TILE
        lower = lower_ref[i] - first
        upper = upper_ref[i] - first
        top = None
        for t in range(6 if i == 3 else 5):
            s = matmul(keys(i + t), qt) * SCALE_LOG2
            allowed = place >= lower - t * TILE
            if t >= 4:
                allowed = allowed & (place <= upper - t * TILE)
            s = jnp.where(allowed, s, MASKED)
            s_buf[i % 2, t] = s
            most = jnp.max(s, axis=0, keepdims=True)
            top = most if top is None else jnp.maximum(top, most)
        return top

    def attend(head, i, top):
        tiles = 6 if i == 3 else 5
        rows = pl.ds(2 * i, 2)
        lanes = pl.ds(i * TILE, TILE)
        window = pl.ds(i * TILE, tiles * TILE)
        total = None
        for t in range(tiles):
            p = jnp.exp2(s_buf[i % 2, t] - top)
            p_buf[pl.ds((i + t) * TILE, TILE), lanes] = p.astype(bf16)
            part = jnp.sum(p, axis=0, keepdims=True)
            total = part if total is None else total + part
        share = 1.0 / total
        out = (matmul(vt_win[:, window], p_buf[window, lanes]) * share).astype(bf16)
        o_buf[head, rows] = out.T.reshape(2, PIECE, HD)
        gt = gt_buf[:, lanes].astype(f32)
        delta_buf[i] = jnp.sum(gt * out.astype(f32), axis=0, keepdims=True)
        scaled_buf[i] = share * SCALE
        column = jnp.broadcast_to(share, (8, TILE)).T[:, :1]
        g = g_buf[head, rows].reshape(TILE, HD).astype(f32)
        q = q_buf[head, rows].reshape(TILE, HD).astype(f32)
        gs_buf[lanes] = (g * column).astype(bf16)
        qs_buf[lanes] = (q * (column * SCALE)).astype(bf16)

    def backward_tile(tile):
        blocks = range(max(0, tile - 4), 1 + min(3, tile)) if tile < 8 else range(3, 4)
        rows = pl.ds(tile * TILE, TILE)
        span = pl.ds(blocks[0] * TILE, len(blocks) * TILE)
        v = values(tile)
        dv_acc[tile] += matmul(p_buf[rows, span], gs_buf[span])
        for i in blocks:
            lanes = pl.ds(i * TILE, TILE)
            dp = matmul(v, gt_buf[:, lanes])
            ds_buf[rows, lanes] = p_buf[rows, lanes] * (dp - delta_buf[i]).astype(bf16)
        dk_acc[tile] += matmul(ds_buf[rows, span], qs_buf[span])

    def grad_queries(head, i):
        lanes = pl.ds(i * TILE, TILE)
        window = pl.ds(i * TILE, (6 if i == 3 else 5) * TILE)
        grad = matmul(kt_win[:, window], ds_buf[window, lanes]) * scaled_buf[i]
        gq_buf[head, pl.ds(2 * i, 2)] = grad.astype(bf16).T.reshape(2, PIECE, HD)

    def out_src(kind, head, target):
        return (o_buf, gq_buf)[kind].at[head, target]

    def out_dst(kind, head, source):
        cols = pl.ds(pl.multiple_of(source * 2 * HD + head * HD, HD), HD)
        return (o_hbm, gq_hbm)[kind].at[:, cols]

    def send_out(kind, head, target):
        @pl.when(target == h)
        def _():
            pltpu.make_async_copy(
                out_src(kind, head, target), out_dst(kind, head, h), out_rsem.at[kind, head, h]
            ).start()

        @pl.when(target != h)
        def _():
            pltpu.make_async_remote_copy(
                src_ref=out_src(kind, head, target),
                dst_ref=out_dst(kind, head, h),
                send_sem=out_ssem.at[kind, head, target],
                recv_sem=out_rsem.at[kind, head, h],
                device_id=(c, target),
                device_id_type=MESH,
            ).start()

    def give_back(side, slot):
        return pltpu.make_async_remote_copy(
            src_ref=ret_send.at[side, slot],
            dst_ref=ret_recv.at[side, slot],
            send_sem=ret_ssem.at[side, slot],
            recv_sem=ret_rsem.at[side, slot],
            device_id=(after if slot == 4 else before, h),
            device_id_type=MESH,
        )

    def own_dst(side, source):
        return (gk_hbm, gv_hbm)[side].at[:, pl.ds(pl.multiple_of(source * HD, HD), HD)]

    def send_own(side, target):
        @pl.when(target == h)
        def _():
            pltpu.make_async_copy(
                own_buf.at[side, target], own_dst(side, h), own_rsem.at[side, h]
            ).start()

        @pl.when(target != h)
        def _():
            pltpu.make_async_remote_copy(
                src_ref=own_buf.at[side, target],
                dst_ref=own_dst(side, h),
                send_sem=own_ssem.at[side, target],
                recv_sem=own_rsem.at[side, h],
                device_id=(c, target),
                device_id_type=MESH,
            ).start()

    def send_sum(tile):
        @pl.when(has_after)
        def _():
            for side in range(2):
                give_back(side, tile).wait_recv()

        if tile == 0:
            @pl.when(has_before)
            def _():
                for side in range(2):
                    give_back(side, 4).wait_recv()

        for side in range(2):
            acc = (dk_acc, dv_acc)[side]
            total = acc[4 + tile] + ret_recv[side, tile].astype(f32)
            if tile == 0:
                total += ret_recv[side, 4].astype(f32)
            own_buf[side, 2 * tile : 2 * tile + 2] = total.astype(bf16).reshape(2, PIECE, HD)
            for part in range(2):
                send_own(side, 2 * tile + part)

    def send_back(slot):
        tile = 8 if slot == 4 else slot
        for side in range(2):
            ret_send[side, slot] = (dk_acc, dv_acc)[side][tile].astype(bf16)
            pl.when(has_after if slot == 4 else has_before)(give_back(side, slot).start)

    @pl.loop(0, 2)
    def _(head):
        @pl.loop(0, n)
        def _(source):
            for kind in range(2):
                dst = (q_buf, g_buf)[kind].at[head, source]
                pltpu.make_async_copy(dst, dst, in_rsem.at[2 + 2 * head + kind, source]).wait()

        for pair in ((3, 2), (1, 0)):
            @pl.when(head == 0)
            def _():
                @pl.when(has_before)
                def _():
                    for tile in pair:
                        for piece in (2 * tile, 2 * tile + 1):
                            for side in range(2):
                                forward(side, piece).wait_recv()

                for tile in pair:
                    turn(tile)
                if pair[0] == 3:
                    @pl.when(has_after)
                    def _():
                        for piece in range(2):
                            for side in range(2):
                                ahead(side, piece).wait_recv()

                    turn(8)

            tops = [scores(head, i) for i in pair]
            for i, top in zip(pair, tops):
                attend(head, i, top)
            for i in pair:
                for part in range(2):
                    send_out(0, head, 2 * i + part)

        for group in ((0, 1), (2, 3, 8), (4, 5), (6, 7)):
            for tile in group:
                backward_tile(tile)
            if group[0] < 4:
                @pl.when(head == 1)
                def _():
                    for tile in group:
                        send_back(min(tile, 4))
            else:
                for tile in group:
                    grad_queries(head, tile - 4)
                for tile in group:
                    for part in range(2):
                        send_out(1, head, 2 * (tile - 4) + part)
            if group[0] == 6:
                @pl.when(head == 1)
                def _():
                    for own in range(4):
                        send_sum(own)

    @pl.loop(0, n)
    def _(other):
        for kind in range(2):
            for head in range(2):
                dst = out_dst(kind, head, other)
                pltpu.make_async_copy(dst, dst, out_rsem.at[kind, head, other]).wait()
            dst = own_dst(kind, other)
            pltpu.make_async_copy(dst, dst, own_rsem.at[kind, other]).wait()
            pl.when(has_after)(forward(kind, other).wait_send)

        @pl.when(other != h)
        def _():
            for stream in range(6):
                src = in_src(stream, other)
                pltpu.make_async_copy(src, src, in_ssem.at[stream, other]).wait()
            for kind in range(2):
                for head in range(2):
                    src = out_src(kind, head, other)
                    pltpu.make_async_copy(src, src, out_ssem.at[kind, head, other]).wait()
                src = own_buf.at[kind, other]
                pltpu.make_async_copy(src, src, own_ssem.at[kind, other]).wait()

    for side in range(2):
        for slot in range(5):
            pl.when(has_after if slot == 4 else has_before)(give_back(side, slot).wait_send)
        for piece in range(2):
            pl.when(has_before)(ahead(side, piece).wait_send)


def place_results(*refs):
    sources, places, held, sems = refs[:4], refs[4:8], refs[8:12], refs[12]
    reads = [pltpu.make_async_copy(sources[k], held[k], sems.at[0, k]) for k in range(4)]
    writes = [pltpu.make_async_copy(held[k], places[k], sems.at[1, k]) for k in range(4)]
    for read in reads:
        read.start()
    for read, write in zip(reads, writes):
        read.wait()
        write.start()
    for write in writes:
        write.wait()


def local(queries, key_rows, value_rows, grad_out, doc_start, reach_end):
    dma = pltpu.SemaphoreType.DMA
    hbm = pl.BlockSpec(memory_space=pltpu.HBM)
    results = pl.pallas_call(
        kernel,
        out_shape=[
            jax.ShapeDtypeStruct(queries.shape, bf16),
            jax.ShapeDtypeStruct(queries.shape, bf16),
            jax.ShapeDtypeStruct(key_rows.shape, bf16),
            jax.ShapeDtypeStruct(key_rows.shape, bf16),
        ],
        in_specs=[hbm] * 6,
        out_specs=[hbm, hbm, hbm, hbm],
        scratch_shapes=[
            pltpu.VMEM((4, 1, TILE), jnp.int32),
            pltpu.VMEM((4, 1, TILE), jnp.int32),
            pltpu.VMEM((2, 8, PIECE, HD), bf16),
            pltpu.VMEM((2, 8, PIECE, HD), bf16),
            pltpu.VMEM((18, PIECE, HD), bf16),
            pltpu.VMEM((18, PIECE, HD), bf16),
            pltpu.VMEM((HD, WINDOW), bf16),
            pltpu.VMEM((HD, WINDOW), bf16),
            pltpu.VMEM((2, 6, TILE, TILE), f32),
            pltpu.VMEM((WINDOW, BLK), bf16),
            pltpu.VMEM((WINDOW, BLK), bf16),
            pltpu.VMEM((HD, BLK), bf16),
            pltpu.VMEM((BLK, HD), bf16),
            pltpu.VMEM((BLK, HD), bf16),
            pltpu.VMEM((4, 1, TILE), f32),
            pltpu.VMEM((4, 1, TILE), f32),
            pltpu.VMEM((9, TILE, HD), f32),
            pltpu.VMEM((9, TILE, HD), f32),
            pltpu.VMEM((2, 8, PIECE, HD), bf16),
            pltpu.VMEM((2, 8, PIECE, HD), bf16),
            pltpu.VMEM((2, 5, TILE, HD), bf16),
            pltpu.VMEM((2, 5, TILE, HD), bf16),
            pltpu.VMEM((2, 8, PIECE, HD), bf16),
            pltpu.VMEM((PIECE, 16 * HD), bf16),
            pltpu.VMEM((PIECE, 8 * HD), bf16),
            pltpu.VMEM((PIECE, 8 * HD), bf16),
            pltpu.VMEM((PIECE, 16 * HD), bf16),
            dma((4,)),
            dma((2,)),
            dma((6, 8)),
            dma((6, 8)),
            dma((2, 8)),
            dma((2, 8)),
            dma((2, 2)),
            dma((2, 2)),
            dma((2, 2, 8)),
            dma((2, 2, 8)),
            dma((2, 5)),
            dma((2, 5)),
            dma((2, 8)),
            dma((2, 8)),
        ],
        compiler_params=pltpu.CompilerParams(
            collective_id=0, has_side_effects=True, vmem_limit_bytes=63 * 1024 * 1024
        ),
    )(
        queries, key_rows, value_rows, grad_out,
        doc_start.reshape(4, 1, TILE), reach_end.reshape(4, 1, TILE),
    )
    return pl.pallas_call(
        place_results,
        out_shape=[jax.ShapeDtypeStruct(r.shape, r.dtype) for r in results],
        in_specs=[hbm] * 4,
        out_specs=[hbm] * 4,
        scratch_shapes=[pltpu.VMEM(r.shape, r.dtype) for r in results] + [dma((2, 4))],
        compiler_params=pltpu.CompilerParams(vmem_limit_bytes=63 * 1024 * 1024),
    )(*results)


def solution(mesh):
    rows = P(("ctx", "head"), None)
    return jax.shard_map(
        local,
        mesh=mesh,
        in_specs=(rows, rows, rows, rows, P("ctx"), P("ctx")),
        out_specs=(rows, rows, rows, rows),
        check_vma=False,
    )
```

```python
import jax
import jax.numpy as jnp
from jax import lax
from jax.experimental import pallas as pl
from jax.experimental.pallas import tpu as pltpu
from jax.sharding import PartitionSpec as P

HD = 128
BLK = 1024
PIECE = 128
TILE = 256
WINDOW = 2304
SCALE = 168.0 ** (-0.5)
SCALE_LOG2 = SCALE * 1.4426950408889634
MASKED = -1e30
MESH = pl.DeviceIdType.MESH
f32 = jnp.float32
bf16 = jnp.bfloat16


def matmul(left, right):
    return lax.dot_general(left, right, (((1,), (0,)), ((), ())), preferred_element_type=f32)


def kernel(
    q_hbm, k_hbm, v_hbm, g_hbm, lower_hbm, upper_hbm,
    o_hbm, gq_hbm, gk_hbm, gv_hbm,
    lower_ref, upper_ref, q_buf, g_buf, k_win, v_win, kt_win, vt_win, s_buf, p_buf, ds_buf,
    gt_buf, gs_buf, qs_buf, delta_buf, scaled_buf, dk_acc, dv_acc,
    o_buf, gq_buf, ret_send, ret_recv, own_buf,
    q_own, k_own, v_own, g_own, stage_sem, mark_sem, in_ssem, in_rsem, fwd_ssem, fwd_rsem, ahead_ssem, ahead_rsem,
    out_ssem, out_rsem, ret_ssem, ret_rsem, own_ssem, own_rsem,
):
    n_ctx = lax.axis_size("ctx")
    n = lax.axis_size("head")
    c = lax.axis_index("ctx")
    h = lax.axis_index("head")
    after = lax.rem(c + 1, n_ctx)
    before = lax.rem(c + n_ctx - 1, n_ctx)
    has_after = c < n_ctx - 1
    has_before = c > 0

    stages = [
        pltpu.make_async_copy(src, dst, stage_sem.at[k])
        for k, (src, dst) in enumerate(
            ((k_hbm, k_own), (v_hbm, v_own), (q_hbm, q_own), (g_hbm, g_own))
        )
    ]
    for stage in stages:
        stage.start()

    barrier = pltpu.get_barrier_semaphore()

    @pl.loop(1, n)
    def _(r):
        pl.semaphore_signal(barrier, inc=1, device_id=(c, lax.rem(h + r, n)), device_id_type=MESH)

    @pl.when(has_after)
    def _():
        pl.semaphore_signal(barrier, inc=1, device_id=(after, h), device_id_type=MESH)

    @pl.when(has_before)
    def _():
        pl.semaphore_signal(barrier, inc=1, device_id=(before, h), device_id_type=MESH)

    neighbours = jnp.where(has_after, 1, 0) + jnp.where(has_before, 1, 0)
    pl.semaphore_wait(barrier, n - 1 + neighbours)

    def in_src(stream, target):
        if stream < 2:
            return (k_own, v_own)[stream].at[:, pl.ds(pl.multiple_of(target * HD, HD), HD)]
        head = (stream - 2) // 2
        cols = pl.ds(pl.multiple_of(target * 2 * HD + head * HD, HD), HD)
        return (q_own, g_own)[stream % 2].at[:, cols]

    def in_dst(stream, source):
        if stream < 2:
            return (k_win, v_win)[stream].at[8 + source]
        return (q_buf, g_buf)[stream % 2].at[(stream - 2) // 2, source]

    core = lax.rem(h, 2)
    turns = (((1, 0), (3, 0)), ((1, 1), (3, 1)), ((2, 0), (2, 1)), ((0, 1),))

    def partner(step, other):
        chip = lax.rem(h // 2 + 4 + (1 - 2 * core) * step, 4)
        return 2 * chip + (1 - core if other else core)

    def send_in(streams, which):
        for turn_of in which:
            for stream in streams:
                for step, other in turn_of:
                    target = partner(step, other)
                    pltpu.make_async_remote_copy(
                        src_ref=in_src(stream, target),
                        dst_ref=in_dst(stream, h),
                        send_sem=in_ssem.at[stream, target],
                        recv_sem=in_rsem.at[stream, h],
                        device_id=(c, target),
                        device_id_type=MESH,
                    ).start()

    def keep_in(streams):
        for stream in streams:
            pltpu.make_async_copy(
                in_src(stream, h), in_dst(stream, h), in_rsem.at[stream, h]
            ).start()

    def wait_in(stream, source):
        dst = in_dst(stream, source)
        pltpu.make_async_copy(dst, dst, in_rsem.at[stream, source]).wait()

    def forward(side, piece):
        win = (k_win, v_win)[side]
        return pltpu.make_async_remote_copy(
            src_ref=win.at[8 + piece],
            dst_ref=win.at[piece],
            send_sem=fwd_ssem.at[side, piece],
            recv_sem=fwd_rsem.at[side, piece],
            device_id=(after, h),
            device_id_type=MESH,
        )

    def ahead(side, piece):
        win = (k_win, v_win)[side]
        return pltpu.make_async_remote_copy(
            src_ref=win.at[8 + piece],
            dst_ref=win.at[16 + piece],
            send_sem=ahead_ssem.at[side, piece],
            recv_sem=ahead_rsem.at[side, piece],
            device_id=(before, h),
            device_id_type=MESH,
        )

    marks = [
        pltpu.make_async_copy(src, dst, mark_sem.at[k])
        for k, (src, dst) in enumerate(((lower_hbm, lower_ref), (upper_hbm, upper_ref)))
    ]
    for mark in marks:
        mark.start()
    stages[0].wait()
    stages[1].wait()
    send_in((0, 1), turns)
    keep_in((0, 1))
    stages[2].wait()
    stages[3].wait()
    send_in((2, 3), turns[:1])
    keep_in((2, 3, 4, 5))
    for place_in, piece in enumerate((7, 6, 0, 1, 5, 4, 3, 2)):
        if place_in in (2, 4, 6):
            send_in((2, 3), turns[place_in // 2 : place_in // 2 + 1])
        for side in range(2):
            wait_in(side, piece)
            if piece >= 2:
                pl.when(has_after)(forward(side, piece).start)
            else:
                pl.when(has_before)(ahead(side, piece).start)

    @pl.when(has_after)
    def _():
        for piece in (1, 0):
            for side in range(2):
                forward(side, piece).start()

    send_in((4, 5), turns)

    @pl.when(jnp.logical_not(has_before))
    def _():
        for side in range(2):
            (k_win, v_win)[side][0:8] = jnp.zeros((8, PIECE, HD), bf16)
            ret_recv[side, 4] = jnp.zeros((TILE, HD), bf16)

    @pl.when(jnp.logical_not(has_after))
    def _():
        for side in range(2):
            (k_win, v_win)[side][16:18] = jnp.zeros((2, PIECE, HD), bf16)
            ret_recv[side, 0:4] = jnp.zeros((4, TILE, HD), bf16)

    for mark in marks:
        mark.wait()
    def keys(tile):
        return k_win[2 * tile : 2 * tile + 2].reshape(TILE, HD)

    def values(tile):
        return v_win[2 * tile : 2 * tile + 2].reshape(TILE, HD)

    def turn(tile):
        rows = pl.ds(tile * TILE, TILE)
        kt_win[:, rows] = keys(tile).T
        vt_win[:, rows] = values(tile).T

    for tile in range(4, 8):
        turn(tile)
    dk_acc[...] = jnp.zeros_like(dk_acc)
    dv_acc[...] = jnp.zeros_like(dv_acc)
    place = lax.broadcasted_iota(jnp.int32, (TILE, TILE), 0)

    def scores(head, i):
        rows = pl.ds(2 * i, 2)
        qt = q_buf[head, rows].reshape(TILE, HD).T
        gt_buf[:, pl.ds(i * TILE, TILE)] = g_buf[head, rows].reshape(TILE, HD).T
        first = (c - 1) * BLK + i * TILE
        lower = lower_ref[i] - first
        upper = upper_ref[i] - first
        top = None
        for t in range(6 if i == 3 else 5):
            s = matmul(keys(i + t), qt) * SCALE_LOG2
            allowed = place >= lower - t * TILE
            if t >= 4:
                allowed = allowed & (place <= upper - t * TILE)
            s = jnp.where(allowed, s, MASKED)
            s_buf[i % 2, t] = s
            most = jnp.max(s, axis=0, keepdims=True)
            top = most if top is None else jnp.maximum(top, most)
        return top

    def attend(head, i, top):
        tiles = 6 if i == 3 else 5
        rows = pl.ds(2 * i, 2)
        lanes = pl.ds(i * TILE, TILE)
        window = pl.ds(i * TILE, tiles * TILE)
        total = None
        for t in range(tiles):
            p = jnp.exp2(s_buf[i % 2, t] - top)
            p_buf[pl.ds((i + t) * TILE, TILE), lanes] = p.astype(bf16)
            part = jnp.sum(p, axis=0, keepdims=True)
            total = part if total is None else total + part
        share = 1.0 / total
        out = (matmul(vt_win[:, window], p_buf[window, lanes]) * share).astype(bf16)
        o_buf[head, rows] = out.T.reshape(2, PIECE, HD)
        gt = gt_buf[:, lanes].astype(f32)
        delta_buf[i] = jnp.sum(gt * out.astype(f32), axis=0, keepdims=True)
        scaled_buf[i] = share * SCALE
        column = jnp.broadcast_to(share, (8, TILE)).T[:, :1]
        g = g_buf[head, rows].reshape(TILE, HD).astype(f32)
        q = q_buf[head, rows].reshape(TILE, HD).astype(f32)
        gs_buf[lanes] = (g * column).astype(bf16)
        qs_buf[lanes] = (q * (column * SCALE)).astype(bf16)

    def backward_tile(tile):
        blocks = range(max(0, tile - 4), 1 + min(3, tile)) if tile < 8 else range(3, 4)
        rows = pl.ds(tile * TILE, TILE)
        span = pl.ds(blocks[0] * TILE, len(blocks) * TILE)
        v = values(tile)
        dv_acc[tile] += matmul(p_buf[rows, span], gs_buf[span])
        for i in blocks:
            lanes = pl.ds(i * TILE, TILE)
            dp = matmul(v, gt_buf[:, lanes])
            ds_buf[rows, lanes] = p_buf[rows, lanes] * (dp - delta_buf[i]).astype(bf16)
        dk_acc[tile] += matmul(ds_buf[rows, span], qs_buf[span])

    def grad_queries(head, i):
        lanes = pl.ds(i * TILE, TILE)
        window = pl.ds(i * TILE, (6 if i == 3 else 5) * TILE)
        grad = matmul(kt_win[:, window], ds_buf[window, lanes]) * scaled_buf[i]
        gq_buf[head, pl.ds(2 * i, 2)] = grad.astype(bf16).T.reshape(2, PIECE, HD)

    def out_src(kind, head, target):
        return (o_buf, gq_buf)[kind].at[head, target]

    def out_dst(kind, head, source):
        cols = pl.ds(pl.multiple_of(source * 2 * HD + head * HD, HD), HD)
        return (o_hbm, gq_hbm)[kind].at[:, cols]

    def send_out(kind, head):
        pltpu.make_async_copy(
            out_src(kind, head, h), out_dst(kind, head, h), out_rsem.at[kind, head, h]
        ).start()
        for turn_of in turns:
            for step, other in turn_of:
                target = partner(step, other)
                pltpu.make_async_remote_copy(
                    src_ref=out_src(kind, head, target),
                    dst_ref=out_dst(kind, head, h),
                    send_sem=out_ssem.at[kind, head, target],
                    recv_sem=out_rsem.at[kind, head, h],
                    device_id=(c, target),
                    device_id_type=MESH,
                ).start()

    def give_back(side, slot):
        return pltpu.make_async_remote_copy(
            src_ref=ret_send.at[side, slot],
            dst_ref=ret_recv.at[side, slot],
            send_sem=ret_ssem.at[side, slot],
            recv_sem=ret_rsem.at[side, slot],
            device_id=(after if slot == 4 else before, h),
            device_id_type=MESH,
        )

    def own_dst(side, source):
        return (gk_hbm, gv_hbm)[side].at[:, pl.ds(pl.multiple_of(source * HD, HD), HD)]

    def send_own():
        for side in range(2):
            pltpu.make_async_copy(own_buf.at[side, h], own_dst(side, h), own_rsem.at[side, h]).start()
        for turn_of in turns:
            for side in range(2):
                for step, other in turn_of:
                    target = partner(step, other)
                    pltpu.make_async_remote_copy(
                        src_ref=own_buf.at[side, target],
                        dst_ref=own_dst(side, h),
                        send_sem=own_ssem.at[side, target],
                        recv_sem=own_rsem.at[side, h],
                        device_id=(c, target),
                        device_id_type=MESH,
                    ).start()

    def add_up(tile):
        @pl.when(has_after)
        def _():
            for side in range(2):
                give_back(side, tile).wait_recv()

        if tile == 0:
            @pl.when(has_before)
            def _():
                for side in range(2):
                    give_back(side, 4).wait_recv()

        for side in range(2):
            acc = (dk_acc, dv_acc)[side]
            total = acc[4 + tile] + ret_recv[side, tile].astype(f32)
            if tile == 0:
                total += ret_recv[side, 4].astype(f32)
            own_buf[side, 2 * tile : 2 * tile + 2] = total.astype(bf16).reshape(2, PIECE, HD)

    def send_back(slot):
        tile = 8 if slot == 4 else slot
        for side in range(2):
            ret_send[side, slot] = (dk_acc, dv_acc)[side][tile].astype(bf16)
            pl.when(has_after if slot == 4 else has_before)(give_back(side, slot).start)

    @pl.loop(0, 2)
    def _(head):
        @pl.loop(0, n)
        def _(source):
            for kind in range(2):
                dst = (q_buf, g_buf)[kind].at[head, source]
                pltpu.make_async_copy(dst, dst, in_rsem.at[2 + 2 * head + kind, source]).wait()

        for pair in ((3, 2), (1, 0)):
            @pl.when(head == 0)
            def _():
                @pl.when(has_before)
                def _():
                    for tile in pair:
                        for piece in (2 * tile, 2 * tile + 1):
                            for side in range(2):
                                forward(side, piece).wait_recv()

                for tile in pair:
                    turn(tile)
                if pair[0] == 3:
                    @pl.when(has_after)
                    def _():
                        for piece in range(2):
                            for side in range(2):
                                ahead(side, piece).wait_recv()

                    turn(8)

            tops = [scores(head, i) for i in pair]
            for i, top in zip(pair, tops):
                attend(head, i, top)

        send_out(0, head)
        for group in ((0, 1), (2, 3, 8), (4, 5), (6, 7)):
            for tile in group:
                backward_tile(tile)
            if group[0] < 4:
                @pl.when(head == 1)
                def _():
                    for tile in group:
                        send_back(min(tile, 4))
            else:
                for tile in group:
                    grad_queries(head, tile - 4)

        send_out(1, head)

    for tile in range(4):
        add_up(tile)
    send_own()

    @pl.loop(0, n)
    def _(other):
        for kind in range(2):
            for head in range(2):
                dst = out_dst(kind, head, other)
                pltpu.make_async_copy(dst, dst, out_rsem.at[kind, head, other]).wait()
            dst = own_dst(kind, other)
            pltpu.make_async_copy(dst, dst, own_rsem.at[kind, other]).wait()
            pl.when(has_after)(forward(kind, other).wait_send)

        @pl.when(other != h)
        def _():
            for stream in range(6):
                src = in_src(stream, other)
                pltpu.make_async_copy(src, src, in_ssem.at[stream, other]).wait()
            for kind in range(2):
                for head in range(2):
                    src = out_src(kind, head, other)
                    pltpu.make_async_copy(src, src, out_ssem.at[kind, head, other]).wait()
                src = own_buf.at[kind, other]
                pltpu.make_async_copy(src, src, own_ssem.at[kind, other]).wait()

    for side in range(2):
        for slot in range(5):
            pl.when(has_after if slot == 4 else has_before)(give_back(side, slot).wait_send)
        for piece in range(2):
            pl.when(has_before)(ahead(side, piece).wait_send)


def place_results(*refs):
    sources, places, held, sems = refs[:4], refs[4:8], refs[8:12], refs[12]
    reads = [pltpu.make_async_copy(sources[k], held[k], sems.at[0, k]) for k in range(4)]
    writes = [pltpu.make_async_copy(held[k], places[k], sems.at[1, k]) for k in range(4)]
    for read in reads:
        read.start()
    for read, write in zip(reads, writes):
        read.wait()
        write.start()
    for write in writes:
        write.wait()


def local(queries, key_rows, value_rows, grad_out, doc_start, reach_end):
    dma = pltpu.SemaphoreType.DMA
    hbm = pl.BlockSpec(memory_space=pltpu.HBM)
    results = pl.pallas_call(
        kernel,
        out_shape=[
            jax.ShapeDtypeStruct(queries.shape, bf16),
            jax.ShapeDtypeStruct(queries.shape, bf16),
            jax.ShapeDtypeStruct(key_rows.shape, bf16),
            jax.ShapeDtypeStruct(key_rows.shape, bf16),
        ],
        in_specs=[hbm] * 6,
        out_specs=[hbm, hbm, hbm, hbm],
        scratch_shapes=[
            pltpu.VMEM((4, 1, TILE), jnp.int32),
            pltpu.VMEM((4, 1, TILE), jnp.int32),
            pltpu.VMEM((2, 8, PIECE, HD), bf16),
            pltpu.VMEM((2, 8, PIECE, HD), bf16),
            pltpu.VMEM((18, PIECE, HD), bf16),
            pltpu.VMEM((18, PIECE, HD), bf16),
            pltpu.VMEM((HD, WINDOW), bf16),
            pltpu.VMEM((HD, WINDOW), bf16),
            pltpu.VMEM((2, 6, TILE, TILE), f32),
            pltpu.VMEM((WINDOW, BLK), bf16),
            pltpu.VMEM((WINDOW, BLK), bf16),
            pltpu.VMEM((HD, BLK), bf16),
            pltpu.VMEM((BLK, HD), bf16),
            pltpu.VMEM((BLK, HD), bf16),
            pltpu.VMEM((4, 1, TILE), f32),
            pltpu.VMEM((4, 1, TILE), f32),
            pltpu.VMEM((9, TILE, HD), f32),
            pltpu.VMEM((9, TILE, HD), f32),
            pltpu.VMEM((2, 8, PIECE, HD), bf16),
            pltpu.VMEM((2, 8, PIECE, HD), bf16),
            pltpu.VMEM((2, 5, TILE, HD), bf16),
            pltpu.VMEM((2, 5, TILE, HD), bf16),
            pltpu.VMEM((2, 8, PIECE, HD), bf16),
            pltpu.VMEM((PIECE, 16 * HD), bf16),
            pltpu.VMEM((PIECE, 8 * HD), bf16),
            pltpu.VMEM((PIECE, 8 * HD), bf16),
            pltpu.VMEM((PIECE, 16 * HD), bf16),
            dma((4,)),
            dma((2,)),
            dma((6, 8)),
            dma((6, 8)),
            dma((2, 8)),
            dma((2, 8)),
            dma((2, 2)),
            dma((2, 2)),
            dma((2, 2, 8)),
            dma((2, 2, 8)),
            dma((2, 5)),
            dma((2, 5)),
            dma((2, 8)),
            dma((2, 8)),
        ],
        compiler_params=pltpu.CompilerParams(
            collective_id=0, has_side_effects=True, vmem_limit_bytes=63 * 1024 * 1024
        ),
    )(
        queries, key_rows, value_rows, grad_out,
        doc_start.reshape(4, 1, TILE), reach_end.reshape(4, 1, TILE),
    )
    return pl.pallas_call(
        place_results,
        out_shape=[jax.ShapeDtypeStruct(r.shape, r.dtype) for r in results],
        in_specs=[hbm] * 4,
        out_specs=[hbm] * 4,
        scratch_shapes=[pltpu.VMEM(r.shape, r.dtype) for r in results] + [dma((2, 4))],
        compiler_params=pltpu.CompilerParams(vmem_limit_bytes=63 * 1024 * 1024),
    )(*results)


def solution(mesh):
    rows = P(("ctx", "head"), None)
    return jax.shard_map(
        local,
        mesh=mesh,
        in_specs=(rows, rows, rows, rows, P("ctx"), P("ctx")),
        out_specs=(rows, rows, rows, rows),
        check_vma=False,
    )
```

```python
import jax
import jax.numpy as jnp
from jax import lax
from jax.experimental import pallas as pl
from jax.experimental.pallas import tpu as pltpu
from jax.sharding import PartitionSpec as P

HD = 128
BLK = 1024
PIECE = 128
TILE = 256
WINDOW = 2304
SCALE = 168.0 ** (-0.5)
SCALE_LOG2 = SCALE * 1.4426950408889634
MASKED = -1e30
MESH = pl.DeviceIdType.MESH
f32 = jnp.float32
bf16 = jnp.bfloat16


def matmul(left, right):
    return lax.dot_general(left, right, (((1,), (0,)), ((), ())), preferred_element_type=f32)


def kernel(
    q_hbm, k_hbm, v_hbm, g_hbm, lower_hbm, upper_hbm,
    o_hbm, gq_hbm, gk_hbm, gv_hbm,
    lower_ref, upper_ref, q_buf, g_buf, k_win, v_win, kt_win, vt_win, s_buf, p_buf, ds_buf,
    gt_buf, gs_buf, qs_buf, delta_buf, scaled_buf, dk_acc, dv_acc,
    o_buf, gq_buf, ret_send, ret_recv, own_buf,
    q_own, k_own, v_own, g_own, stage_sem, mark_sem, in_ssem, in_rsem, fwd_ssem, fwd_rsem, ahead_ssem, ahead_rsem,
    out_ssem, out_rsem, ret_ssem, ret_rsem, own_ssem, own_rsem,
):
    n_ctx = lax.axis_size("ctx")
    n = lax.axis_size("head")
    c = lax.axis_index("ctx")
    h = lax.axis_index("head")
    after = lax.rem(c + 1, n_ctx)
    before = lax.rem(c + n_ctx - 1, n_ctx)
    has_after = c < n_ctx - 1
    has_before = c > 0

    stages = [
        pltpu.make_async_copy(src, dst, stage_sem.at[k])
        for k, (src, dst) in enumerate(
            ((k_hbm, k_own), (v_hbm, v_own), (q_hbm, q_own), (g_hbm, g_own))
        )
    ]
    for stage in stages:
        stage.start()

    barrier = pltpu.get_barrier_semaphore()

    @pl.loop(1, n)
    def _(r):
        pl.semaphore_signal(barrier, inc=1, device_id=(c, lax.rem(h + r, n)), device_id_type=MESH)

    @pl.when(has_after)
    def _():
        pl.semaphore_signal(barrier, inc=1, device_id=(after, h), device_id_type=MESH)

    @pl.when(has_before)
    def _():
        pl.semaphore_signal(barrier, inc=1, device_id=(before, h), device_id_type=MESH)

    neighbours = jnp.where(has_after, 1, 0) + jnp.where(has_before, 1, 0)
    pl.semaphore_wait(barrier, n - 1 + neighbours)

    def in_src(stream, target):
        if stream < 2:
            return (k_own, v_own)[stream].at[:, pl.ds(pl.multiple_of(target * HD, HD), HD)]
        head = (stream - 2) // 2
        cols = pl.ds(pl.multiple_of(target * 2 * HD + head * HD, HD), HD)
        return (q_own, g_own)[stream % 2].at[:, cols]

    def in_dst(stream, source):
        if stream < 2:
            return (k_win, v_win)[stream].at[8 + source]
        return (q_buf, g_buf)[stream % 2].at[(stream - 2) // 2, source]

    def send_in(streams):
        for stream in streams:
            pltpu.make_async_copy(
                in_src(stream, h), in_dst(stream, h), in_rsem.at[stream, h]
            ).start()

        @pl.loop(1, n)
        def _(r):
            target = lax.rem(h + r, n)
            for stream in streams:
                pltpu.make_async_remote_copy(
                    src_ref=in_src(stream, target),
                    dst_ref=in_dst(stream, h),
                    send_sem=in_ssem.at[stream, target],
                    recv_sem=in_rsem.at[stream, h],
                    device_id=(c, target),
                    device_id_type=MESH,
                ).start()

    def wait_in(stream, source):
        dst = in_dst(stream, source)
        pltpu.make_async_copy(dst, dst, in_rsem.at[stream, source]).wait()

    def forward(side, piece):
        win = (k_win, v_win)[side]
        return pltpu.make_async_remote_copy(
            src_ref=win.at[8 + piece],
            dst_ref=win.at[piece],
            send_sem=fwd_ssem.at[side, piece],
            recv_sem=fwd_rsem.at[side, piece],
            device_id=(after, h),
            device_id_type=MESH,
        )

    def ahead(side, piece):
        win = (k_win, v_win)[side]
        return pltpu.make_async_remote_copy(
            src_ref=win.at[8 + piece],
            dst_ref=win.at[16 + piece],
            send_sem=ahead_ssem.at[side, piece],
            recv_sem=ahead_rsem.at[side, piece],
            device_id=(before, h),
            device_id_type=MESH,
        )

    marks = [
        pltpu.make_async_copy(src, dst, mark_sem.at[k])
        for k, (src, dst) in enumerate(((lower_hbm, lower_ref), (upper_hbm, upper_ref)))
    ]
    for mark in marks:
        mark.start()
    stages[0].wait()
    stages[1].wait()
    send_in((0, 1))
    stages[2].wait()
    stages[3].wait()
    send_in((2, 3))
    for piece in (7, 6, 0, 1, 5, 4, 3, 2):
        for side in range(2):
            wait_in(side, piece)
            if piece >= 2:
                pl.when(has_after)(forward(side, piece).start)
            else:
                pl.when(has_before)(ahead(side, piece).start)

    @pl.when(has_after)
    def _():
        for piece in (1, 0):
            for side in range(2):
                forward(side, piece).start()

    send_in((4, 5))

    @pl.when(jnp.logical_not(has_before))
    def _():
        for side in range(2):
            (k_win, v_win)[side][0:8] = jnp.zeros((8, PIECE, HD), bf16)
            ret_recv[side, 4] = jnp.zeros((TILE, HD), bf16)

    @pl.when(jnp.logical_not(has_after))
    def _():
        for side in range(2):
            (k_win, v_win)[side][16:18] = jnp.zeros((2, PIECE, HD), bf16)
            ret_recv[side, 0:4] = jnp.zeros((4, TILE, HD), bf16)

    for mark in marks:
        mark.wait()
    def keys(tile):
        return k_win[2 * tile : 2 * tile + 2].reshape(TILE, HD)

    def values(tile):
        return v_win[2 * tile : 2 * tile + 2].reshape(TILE, HD)

    def turn(tile):
        rows = pl.ds(tile * TILE, TILE)
        kt_win[:, rows] = keys(tile).T
        vt_win[:, rows] = values(tile).T

    for tile in range(4, 8):
        turn(tile)
    dk_acc[...] = jnp.zeros_like(dk_acc)
    dv_acc[...] = jnp.zeros_like(dv_acc)
    place = lax.broadcasted_iota(jnp.int32, (TILE, TILE), 0)

    def scores(head, i):
        rows = pl.ds(2 * i, 2)
        qt = q_buf[head, rows].reshape(TILE, HD).T
        gt_buf[head, :, pl.ds(i * TILE, TILE)] = g_buf[head, rows].reshape(TILE, HD).T
        first = (c - 1) * BLK + i * TILE
        lower = lower_ref[i] - first
        upper = upper_ref[i] - first
        top = None
        for t in range(6 if i == 3 else 5):
            s = matmul(keys(i + t), qt) * SCALE_LOG2
            allowed = place >= lower - t * TILE
            if t >= 4:
                allowed = allowed & (place <= upper - t * TILE)
            s = jnp.where(allowed, s, MASKED)
            s_buf[i % 2, t] = s
            most = jnp.max(s, axis=0, keepdims=True)
            top = most if top is None else jnp.maximum(top, most)
        return top

    def attend(head, i, top):
        tiles = 6 if i == 3 else 5
        rows = pl.ds(2 * i, 2)
        lanes = pl.ds(i * TILE, TILE)
        window = pl.ds(i * TILE, tiles * TILE)
        total = None
        for t in range(tiles):
            p = jnp.exp2(s_buf[i % 2, t] - top)
            p_buf[head, pl.ds((i + t) * TILE, TILE), lanes] = p.astype(bf16)
            part = jnp.sum(p, axis=0, keepdims=True)
            total = part if total is None else total + part
        share = 1.0 / total
        out = (matmul(vt_win[:, window], p_buf[head, window, lanes]) * share).astype(bf16)
        o_buf[head, rows] = out.T.reshape(2, PIECE, HD)
        gt = gt_buf[head, :, lanes].astype(f32)
        delta_buf[head, i] = jnp.sum(gt * out.astype(f32), axis=0, keepdims=True)
        scaled_buf[head, i] = share * SCALE
        column = jnp.broadcast_to(share, (8, TILE)).T[:, :1]
        g = g_buf[head, rows].reshape(TILE, HD).astype(f32)
        q = q_buf[head, rows].reshape(TILE, HD).astype(f32)
        gs_buf[head, lanes] = (g * column).astype(bf16)
        qs_buf[head, lanes] = (q * (column * SCALE)).astype(bf16)

    def backward_tile(head, tile, blocks=range(4)):
        reach = range(max(0, tile - 4), 1 + min(3, tile)) if tile < 8 else range(3, 4)
        blocks = [i for i in reach if i in blocks]
        rows = pl.ds(tile * TILE, TILE)
        span = pl.ds(blocks[0] * TILE, len(blocks) * TILE)
        v = values(tile)
        dv_acc[tile] += matmul(p_buf[head, rows, span], gs_buf[head, span])
        for i in blocks:
            lanes = pl.ds(i * TILE, TILE)
            dp = matmul(v, gt_buf[head, :, lanes])
            ds_buf[head, rows, lanes] = p_buf[head, rows, lanes] * (
                dp - delta_buf[head, i]
            ).astype(bf16)
        dk_acc[tile] += matmul(ds_buf[head, rows, span], qs_buf[head, span])

    def grad_queries(head, i):
        lanes = pl.ds(i * TILE, TILE)
        window = pl.ds(i * TILE, (6 if i == 3 else 5) * TILE)
        grad = matmul(kt_win[:, window], ds_buf[head, window, lanes]) * scaled_buf[head, i]
        gq_buf[head, pl.ds(2 * i, 2)] = grad.astype(bf16).T.reshape(2, PIECE, HD)

    def out_src(kind, head, target):
        return (o_buf, gq_buf)[kind].at[head, target]

    def out_dst(kind, head, source):
        cols = pl.ds(pl.multiple_of(source * 2 * HD + head * HD, HD), HD)
        return (o_hbm, gq_hbm)[kind].at[:, cols]

    def send_out(kind, head, target):
        @pl.when(target == h)
        def _():
            pltpu.make_async_copy(
                out_src(kind, head, target), out_dst(kind, head, h), out_rsem.at[kind, head, h]
            ).start()

        @pl.when(target != h)
        def _():
            pltpu.make_async_remote_copy(
                src_ref=out_src(kind, head, target),
                dst_ref=out_dst(kind, head, h),
                send_sem=out_ssem.at[kind, head, target],
                recv_sem=out_rsem.at[kind, head, h],
                device_id=(c, target),
                device_id_type=MESH,
            ).start()

    def give_back(side, slot):
        return pltpu.make_async_remote_copy(
            src_ref=ret_send.at[side, slot],
            dst_ref=ret_recv.at[side, slot],
            send_sem=ret_ssem.at[side, slot],
            recv_sem=ret_rsem.at[side, slot],
            device_id=(after if slot == 4 else before, h),
            device_id_type=MESH,
        )

    def own_dst(side, source):
        return (gk_hbm, gv_hbm)[side].at[:, pl.ds(pl.multiple_of(source * HD, HD), HD)]

    def send_own(side, target):
        @pl.when(target == h)
        def _():
            pltpu.make_async_copy(
                own_buf.at[side, target], own_dst(side, h), own_rsem.at[side, h]
            ).start()

        @pl.when(target != h)
        def _():
            pltpu.make_async_remote_copy(
                src_ref=own_buf.at[side, target],
                dst_ref=own_dst(side, h),
                send_sem=own_ssem.at[side, target],
                recv_sem=own_rsem.at[side, h],
                device_id=(c, target),
                device_id_type=MESH,
            ).start()

    def send_sum(tile):
        @pl.when(has_after)
        def _():
            for side in range(2):
                give_back(side, tile).wait_recv()

        if tile == 0:
            @pl.when(has_before)
            def _():
                for side in range(2):
                    give_back(side, 4).wait_recv()

        for side in range(2):
            acc = (dk_acc, dv_acc)[side]
            total = acc[4 + tile] + ret_recv[side, tile].astype(f32)
            if tile == 0:
                total += ret_recv[side, 4].astype(f32)
            own_buf[side, 2 * tile : 2 * tile + 2] = total.astype(bf16).reshape(2, PIECE, HD)
            for part in range(2):
                send_own(side, 2 * tile + part)

    def send_back(slot):
        tile = 8 if slot == 4 else slot
        for side in range(2):
            ret_send[side, slot] = (dk_acc, dv_acc)[side][tile].astype(bf16)
            pl.when(has_after if slot == 4 else has_before)(give_back(side, slot).start)

    def wait_head(head):
        @pl.loop(0, n)
        def _(source):
            for kind in range(2):
                wait_in(2 + 2 * head + kind, source)

    def wait_prior(tiles):
        @pl.when(has_before)
        def _():
            for tile in tiles:
                for piece in (2 * tile, 2 * tile + 1):
                    for side in range(2):
                        forward(side, piece).wait_recv()

        for tile in tiles:
            turn(tile)

    def forward_pair(head, pair):
        tops = [scores(head, i) for i in pair]
        for i, top in zip(pair, tops):
            attend(head, i, top)
        for i in pair:
            for part in range(2):
                send_out(0, head, 2 * i + part)

    def send_grad(head, blocks):
        for i in blocks:
            for part in range(2):
                send_out(1, head, 2 * i + part)

    wait_head(0)
    wait_prior((3, 2))

    @pl.when(has_after)
    def _():
        for piece in range(2):
            for side in range(2):
                ahead(side, piece).wait_recv()

    turn(8)
    forward_pair(0, (3, 2))
    for tile in (8, 4, 5, 6, 7):
        backward_tile(0, tile, (2, 3))
    wait_prior((1, 0))
    forward_pair(0, (1, 0))
    wait_head(1)
    forward_pair(1, (3, 2))
    forward_pair(1, (1, 0))
    for group in ((0, 1), (2,), (3, 8)):
        for tile in group:
            if tile < 8:
                backward_tile(0, tile)
            backward_tile(1, tile)
        for tile in group:
            send_back(min(tile, 4))
    backward_tile(0, 4, (0, 1))
    backward_tile(0, 5, (1,))
    for i in range(4):
        grad_queries(0, i)
    send_grad(0, range(4))
    backward_tile(1, 4)
    backward_tile(1, 5)
    grad_queries(1, 0)
    grad_queries(1, 1)
    send_grad(1, (0, 1))
    backward_tile(1, 6)
    backward_tile(1, 7)
    grad_queries(1, 2)
    grad_queries(1, 3)
    send_grad(1, (2, 3))
    for tile in range(4):
        send_sum(tile)

    @pl.loop(0, n)
    def _(other):
        for kind in range(2):
            for head in range(2):
                dst = out_dst(kind, head, other)
                pltpu.make_async_copy(dst, dst, out_rsem.at[kind, head, other]).wait()
            dst = own_dst(kind, other)
            pltpu.make_async_copy(dst, dst, own_rsem.at[kind, other]).wait()
            pl.when(has_after)(forward(kind, other).wait_send)

        @pl.when(other != h)
        def _():
            for stream in range(6):
                src = in_src(stream, other)
                pltpu.make_async_copy(src, src, in_ssem.at[stream, other]).wait()
            for kind in range(2):
                for head in range(2):
                    src = out_src(kind, head, other)
                    pltpu.make_async_copy(src, src, out_ssem.at[kind, head, other]).wait()
                src = own_buf.at[kind, other]
                pltpu.make_async_copy(src, src, own_ssem.at[kind, other]).wait()

    for side in range(2):
        for slot in range(5):
            pl.when(has_after if slot == 4 else has_before)(give_back(side, slot).wait_send)
        for piece in range(2):
            pl.when(has_before)(ahead(side, piece).wait_send)


def place_results(*refs):
    sources, places, held, sems = refs[:4], refs[4:8], refs[8:12], refs[12]
    reads = [pltpu.make_async_copy(sources[k], held[k], sems.at[0, k]) for k in range(4)]
    writes = [pltpu.make_async_copy(held[k], places[k], sems.at[1, k]) for k in range(4)]
    for read in reads:
        read.start()
    for read, write in zip(reads, writes):
        read.wait()
        write.start()
    for write in writes:
        write.wait()


def local(queries, key_rows, value_rows, grad_out, doc_start, reach_end):
    dma = pltpu.SemaphoreType.DMA
    hbm = pl.BlockSpec(memory_space=pltpu.HBM)
    results = pl.pallas_call(
        kernel,
        out_shape=[
            jax.ShapeDtypeStruct(queries.shape, bf16),
            jax.ShapeDtypeStruct(queries.shape, bf16),
            jax.ShapeDtypeStruct(key_rows.shape, bf16),
            jax.ShapeDtypeStruct(key_rows.shape, bf16),
        ],
        in_specs=[hbm] * 6,
        out_specs=[hbm, hbm, hbm, hbm],
        scratch_shapes=[
            pltpu.VMEM((4, 1, TILE), jnp.int32),
            pltpu.VMEM((4, 1, TILE), jnp.int32),
            pltpu.VMEM((2, 8, PIECE, HD), bf16),
            pltpu.VMEM((2, 8, PIECE, HD), bf16),
            pltpu.VMEM((18, PIECE, HD), bf16),
            pltpu.VMEM((18, PIECE, HD), bf16),
            pltpu.VMEM((HD, WINDOW), bf16),
            pltpu.VMEM((HD, WINDOW), bf16),
            pltpu.VMEM((2, 6, TILE, TILE), f32),
            pltpu.VMEM((2, WINDOW, BLK), bf16),
            pltpu.VMEM((2, WINDOW, BLK), bf16),
            pltpu.VMEM((2, HD, BLK), bf16),
            pltpu.VMEM((2, BLK, HD), bf16),
            pltpu.VMEM((2, BLK, HD), bf16),
            pltpu.VMEM((2, 4, 1, TILE), f32),
            pltpu.VMEM((2, 4, 1, TILE), f32),
            pltpu.VMEM((9, TILE, HD), f32),
            pltpu.VMEM((9, TILE, HD), f32),
            pltpu.VMEM((2, 8, PIECE, HD), bf16),
            pltpu.VMEM((2, 8, PIECE, HD), bf16),
            pltpu.VMEM((2, 5, TILE, HD), bf16),
            pltpu.VMEM((2, 5, TILE, HD), bf16),
            pltpu.VMEM((2, 8, PIECE, HD), bf16),
            pltpu.VMEM((PIECE, 16 * HD), bf16),
            pltpu.VMEM((PIECE, 8 * HD), bf16),
            pltpu.VMEM((PIECE, 8 * HD), bf16),
            pltpu.VMEM((PIECE, 16 * HD), bf16),
            dma((4,)),
            dma((2,)),
            dma((6, 8)),
            dma((6, 8)),
            dma((2, 8)),
            dma((2, 8)),
            dma((2, 2)),
            dma((2, 2)),
            dma((2, 2, 8)),
            dma((2, 2, 8)),
            dma((2, 5)),
            dma((2, 5)),
            dma((2, 8)),
            dma((2, 8)),
        ],
        compiler_params=pltpu.CompilerParams(
            collective_id=0, has_side_effects=True, vmem_limit_bytes=63 * 1024 * 1024
        ),
    )(
        queries, key_rows, value_rows, grad_out,
        doc_start.reshape(4, 1, TILE), reach_end.reshape(4, 1, TILE),
    )
    return pl.pallas_call(
        place_results,
        out_shape=[jax.ShapeDtypeStruct(r.shape, r.dtype) for r in results],
        in_specs=[hbm] * 4,
        out_specs=[hbm] * 4,
        scratch_shapes=[pltpu.VMEM(r.shape, r.dtype) for r in results] + [dma((2, 4))],
        compiler_params=pltpu.CompilerParams(vmem_limit_bytes=63 * 1024 * 1024),
    )(*results)


def solution(mesh):
    rows = P(("ctx", "head"), None)
    return jax.shard_map(
        local,
        mesh=mesh,
        in_specs=(rows, rows, rows, rows, P("ctx"), P("ctx")),
        out_specs=(rows, rows, rows, rows),
        check_vma=False,
    )
```

```python
import jax
import jax.numpy as jnp
from jax import lax
from jax.experimental import pallas as pl
from jax.experimental.pallas import tpu as pltpu
from jax.sharding import PartitionSpec as P

HD = 128
BLK = 1024
PIECE = 128
TILE = 256
WINDOW = 2304
SCALE = 168.0 ** (-0.5)
SCALE_LOG2 = SCALE * 1.4426950408889634
MASKED = -1e30
MESH = pl.DeviceIdType.MESH
f32 = jnp.float32
bf16 = jnp.bfloat16


def matmul(left, right):
    return lax.dot_general(left, right, (((1,), (0,)), ((), ())), preferred_element_type=f32)


def kernel(
    q_hbm, k_hbm, v_hbm, g_hbm, lower_hbm, upper_hbm,
    o_hbm, gq_hbm, gk_hbm, gv_hbm,
    lower_ref, upper_ref, q_buf, g_buf, k_win, v_win, kt_win, vt_win, s_buf, p_buf, ds_buf,
    gt_buf, gs_buf, qs_buf, delta_buf, scaled_buf, dk_acc, dv_acc,
    o_buf, gq_buf, ret_send, ret_recv, own_buf,
    q_own, k_own, v_own, g_own, stage_sem, mark_sem, in_ssem, in_rsem, fwd_ssem, fwd_rsem, ahead_ssem, ahead_rsem,
    out_ssem, out_rsem, ret_ssem, ret_rsem, own_ssem, own_rsem,
):
    n_ctx = lax.axis_size("ctx")
    n = lax.axis_size("head")
    c = lax.axis_index("ctx")
    h = lax.axis_index("head")
    after = lax.rem(c + 1, n_ctx)
    before = lax.rem(c + n_ctx - 1, n_ctx)
    has_after = c < n_ctx - 1
    has_before = c > 0

    stages = [
        pltpu.make_async_copy(src, dst, stage_sem.at[k])
        for k, (src, dst) in enumerate(
            ((k_hbm, k_own), (v_hbm, v_own), (q_hbm, q_own), (g_hbm, g_own))
        )
    ]
    for stage in stages:
        stage.start()

    barrier = pltpu.get_barrier_semaphore()

    @pl.loop(1, n)
    def _(r):
        pl.semaphore_signal(barrier, inc=1, device_id=(c, lax.rem(h + r, n)), device_id_type=MESH)

    @pl.when(has_after)
    def _():
        pl.semaphore_signal(barrier, inc=1, device_id=(after, h), device_id_type=MESH)

    @pl.when(has_before)
    def _():
        pl.semaphore_signal(barrier, inc=1, device_id=(before, h), device_id_type=MESH)

    neighbours = jnp.where(has_after, 1, 0) + jnp.where(has_before, 1, 0)
    pl.semaphore_wait(barrier, n - 1 + neighbours)

    def in_src(stream, target):
        if stream < 2:
            return (k_own, v_own)[stream].at[:, pl.ds(pl.multiple_of(target * HD, HD), HD)]
        head = (stream - 2) // 2
        cols = pl.ds(pl.multiple_of(target * 2 * HD + head * HD, HD), HD)
        return (q_own, g_own)[stream % 2].at[:, cols]

    def in_dst(stream, source):
        if stream < 2:
            return (k_win, v_win)[stream].at[8 + source]
        return (q_buf, g_buf)[stream % 2].at[(stream - 2) // 2, source]

    def send_in(streams):
        for stream in streams:
            pltpu.make_async_copy(
                in_src(stream, h), in_dst(stream, h), in_rsem.at[stream, h]
            ).start()

        @pl.loop(1, n)
        def _(r):
            target = lax.rem(h + r, n)
            for stream in streams:
                pltpu.make_async_remote_copy(
                    src_ref=in_src(stream, target),
                    dst_ref=in_dst(stream, h),
                    send_sem=in_ssem.at[stream, target],
                    recv_sem=in_rsem.at[stream, h],
                    device_id=(c, target),
                    device_id_type=MESH,
                ).start()

    def wait_in(stream, source):
        dst = in_dst(stream, source)
        pltpu.make_async_copy(dst, dst, in_rsem.at[stream, source]).wait()

    def forward(side, piece):
        win = (k_win, v_win)[side]
        return pltpu.make_async_remote_copy(
            src_ref=win.at[8 + piece],
            dst_ref=win.at[piece],
            send_sem=fwd_ssem.at[side, piece],
            recv_sem=fwd_rsem.at[side, piece],
            device_id=(after, h),
            device_id_type=MESH,
        )

    def ahead(side, piece):
        win = (k_win, v_win)[side]
        return pltpu.make_async_remote_copy(
            src_ref=win.at[8 + piece],
            dst_ref=win.at[16 + piece],
            send_sem=ahead_ssem.at[side, piece],
            recv_sem=ahead_rsem.at[side, piece],
            device_id=(before, h),
            device_id_type=MESH,
        )

    marks = [
        pltpu.make_async_copy(src, dst, mark_sem.at[k])
        for k, (src, dst) in enumerate(((lower_hbm, lower_ref), (upper_hbm, upper_ref)))
    ]
    for mark in marks:
        mark.start()
    stages[0].wait()
    stages[1].wait()

    @pl.when(has_after)
    def _():
        for side in range(2):
            pltpu.make_async_remote_copy(
                src_ref=in_src(side, h),
                dst_ref=(k_win, v_win)[side].at[h],
                send_sem=fwd_ssem.at[side, h],
                recv_sem=fwd_rsem.at[side, h],
                device_id=(after, h),
                device_id_type=MESH,
            ).start()

    send_in((0, 1))
    stages[2].wait()
    stages[3].wait()
    send_in((2, 3))
    for piece in (7, 6, 0, 1, 5, 4, 3, 2):
        for side in range(2):
            wait_in(side, piece)
            if piece >= 2:
                pl.when(has_after & (h != piece))(forward(side, piece).start)
            else:
                pl.when(has_before)(ahead(side, piece).start)

    for piece in (1, 0):
        for side in range(2):
            pl.when(has_after & (h != piece))(forward(side, piece).start)

    send_in((4, 5))

    @pl.when(jnp.logical_not(has_before))
    def _():
        for side in range(2):
            (k_win, v_win)[side][0:8] = jnp.zeros((8, PIECE, HD), bf16)
            ret_recv[side, 4] = jnp.zeros((TILE, HD), bf16)

    @pl.when(jnp.logical_not(has_after))
    def _():
        for side in range(2):
            (k_win, v_win)[side][16:18] = jnp.zeros((2, PIECE, HD), bf16)
            ret_recv[side, 0:4] = jnp.zeros((4, TILE, HD), bf16)

    for mark in marks:
        mark.wait()
    def keys(tile):
        return k_win[2 * tile : 2 * tile + 2].reshape(TILE, HD)

    def values(tile):
        return v_win[2 * tile : 2 * tile + 2].reshape(TILE, HD)

    def turn(tile):
        rows = pl.ds(tile * TILE, TILE)
        kt_win[:, rows] = keys(tile).T
        vt_win[:, rows] = values(tile).T

    for tile in range(4, 8):
        turn(tile)
    dk_acc[...] = jnp.zeros_like(dk_acc)
    dv_acc[...] = jnp.zeros_like(dv_acc)
    place = lax.broadcasted_iota(jnp.int32, (TILE, TILE), 0)

    def scores(head, i):
        rows = pl.ds(2 * i, 2)
        qt = q_buf[head, rows].reshape(TILE, HD).T
        gt_buf[head, :, pl.ds(i * TILE, TILE)] = g_buf[head, rows].reshape(TILE, HD).T
        first = (c - 1) * BLK + i * TILE
        lower = lower_ref[i] - first
        upper = upper_ref[i] - first
        top = None
        for t in range(6 if i == 3 else 5):
            s = matmul(keys(i + t), qt) * SCALE_LOG2
            allowed = place >= lower - t * TILE
            if t >= 4:
                allowed = allowed & (place <= upper - t * TILE)
            s = jnp.where(allowed, s, MASKED)
            s_buf[i % 2, t] = s
            most = jnp.max(s, axis=0, keepdims=True)
            top = most if top is None else jnp.maximum(top, most)
        return top

    def attend(head, i, top):
        tiles = 6 if i == 3 else 5
        rows = pl.ds(2 * i, 2)
        lanes = pl.ds(i * TILE, TILE)
        window = pl.ds(i * TILE, tiles * TILE)
        total = None
        for t in range(tiles):
            p = jnp.exp2(s_buf[i % 2, t] - top)
            p_buf[head, pl.ds((i + t) * TILE, TILE), lanes] = p.astype(bf16)
            part = jnp.sum(p, axis=0, keepdims=True)
            total = part if total is None else total + part
        share = 1.0 / total
        out = (matmul(vt_win[:, window], p_buf[head, window, lanes]) * share).astype(bf16)
        o_buf[head, rows] = out.T.reshape(2, PIECE, HD)
        gt = gt_buf[head, :, lanes].astype(f32)
        delta_buf[head, i] = jnp.sum(gt * out.astype(f32), axis=0, keepdims=True)
        scaled_buf[head, i] = share * SCALE
        column = jnp.broadcast_to(share, (8, TILE)).T[:, :1]
        g = g_buf[head, rows].reshape(TILE, HD).astype(f32)
        q = q_buf[head, rows].reshape(TILE, HD).astype(f32)
        gs_buf[head, lanes] = (g * column).astype(bf16)
        qs_buf[head, lanes] = (q * (column * SCALE)).astype(bf16)

    def backward_tile(head, tile, blocks=range(4)):
        reach = range(max(0, tile - 4), 1 + min(3, tile)) if tile < 8 else range(3, 4)
        blocks = [i for i in reach if i in blocks]
        rows = pl.ds(tile * TILE, TILE)
        span = pl.ds(blocks[0] * TILE, len(blocks) * TILE)
        v = values(tile)
        dv_acc[tile] += matmul(p_buf[head, rows, span], gs_buf[head, span])
        for i in blocks:
            lanes = pl.ds(i * TILE, TILE)
            dp = matmul(v, gt_buf[head, :, lanes])
            ds_buf[head, rows, lanes] = p_buf[head, rows, lanes] * (
                dp - delta_buf[head, i]
            ).astype(bf16)
        dk_acc[tile] += matmul(ds_buf[head, rows, span], qs_buf[head, span])

    def grad_queries(head, i):
        lanes = pl.ds(i * TILE, TILE)
        window = pl.ds(i * TILE, (6 if i == 3 else 5) * TILE)
        grad = matmul(kt_win[:, window], ds_buf[head, window, lanes]) * scaled_buf[head, i]
        gq_buf[head, pl.ds(2 * i, 2)] = grad.astype(bf16).T.reshape(2, PIECE, HD)

    def out_src(kind, head, target):
        return (o_buf, gq_buf)[kind].at[head, target]

    def out_dst(kind, head, source):
        cols = pl.ds(pl.multiple_of(source * 2 * HD + head * HD, HD), HD)
        return (o_hbm, gq_hbm)[kind].at[:, cols]

    def send_out(kind, head, target):
        @pl.when(target == h)
        def _():
            pltpu.make_async_copy(
                out_src(kind, head, target), out_dst(kind, head, h), out_rsem.at[kind, head, h]
            ).start()

        @pl.when(target != h)
        def _():
            pltpu.make_async_remote_copy(
                src_ref=out_src(kind, head, target),
                dst_ref=out_dst(kind, head, h),
                send_sem=out_ssem.at[kind, head, target],
                recv_sem=out_rsem.at[kind, head, h],
                device_id=(c, target),
                device_id_type=MESH,
            ).start()

    def give_back(side, slot):
        return pltpu.make_async_remote_copy(
            src_ref=ret_send.at[side, slot],
            dst_ref=ret_recv.at[side, slot],
            send_sem=ret_ssem.at[side, slot],
            recv_sem=ret_rsem.at[side, slot],
            device_id=(after if slot == 4 else before, h),
            device_id_type=MESH,
        )

    def own_dst(side, source):
        return (gk_hbm, gv_hbm)[side].at[:, pl.ds(pl.multiple_of(source * HD, HD), HD)]

    def send_own(side, target):
        @pl.when(target == h)
        def _():
            pltpu.make_async_copy(
                own_buf.at[side, target], own_dst(side, h), own_rsem.at[side, h]
            ).start()

        @pl.when(target != h)
        def _():
            pltpu.make_async_remote_copy(
                src_ref=own_buf.at[side, target],
                dst_ref=own_dst(side, h),
                send_sem=own_ssem.at[side, target],
                recv_sem=own_rsem.at[side, h],
                device_id=(c, target),
                device_id_type=MESH,
            ).start()

    def send_sum(tile):
        @pl.when(has_after)
        def _():
            for side in range(2):
                give_back(side, tile).wait_recv()

        if tile == 0:
            @pl.when(has_before)
            def _():
                for side in range(2):
                    give_back(side, 4).wait_recv()

        for side in range(2):
            acc = (dk_acc, dv_acc)[side]
            total = acc[4 + tile] + ret_recv[side, tile].astype(f32)
            if tile == 0:
                total += ret_recv[side, 4].astype(f32)
            own_buf[side, 2 * tile : 2 * tile + 2] = total.astype(bf16).reshape(2, PIECE, HD)
            for part in range(2):
                send_own(side, 2 * tile + part)

    def send_back(slot):
        tile = 8 if slot == 4 else slot
        for side in range(2):
            ret_send[side, slot] = (dk_acc, dv_acc)[side][tile].astype(bf16)
            pl.when(has_after if slot == 4 else has_before)(give_back(side, slot).start)

    def wait_head(head):
        @pl.loop(0, n)
        def _(source):
            for kind in range(2):
                wait_in(2 + 2 * head + kind, source)

    def wait_prior(tiles):
        @pl.when(has_before)
        def _():
            for tile in tiles:
                for piece in (2 * tile, 2 * tile + 1):
                    for side in range(2):
                        forward(side, piece).wait_recv()

        for tile in tiles:
            turn(tile)

    def forward_pair(head, pair):
        tops = [scores(head, i) for i in pair]
        for i, top in zip(pair, tops):
            attend(head, i, top)
        for i in pair:
            for part in range(2):
                send_out(0, head, 2 * i + part)

    def send_grad(head, blocks):
        for i in blocks:
            for part in range(2):
                send_out(1, head, 2 * i + part)

    wait_head(0)
    wait_prior((3, 2))

    @pl.when(has_after)
    def _():
        for piece in range(2):
            for side in range(2):
                ahead(side, piece).wait_recv()

    turn(8)
    forward_pair(0, (3, 2))
    for tile in (8, 4, 5, 6, 7):
        backward_tile(0, tile, (2, 3))
    wait_prior((1, 0))
    forward_pair(0, (1, 0))
    backward_tile(0, 0)
    backward_tile(0, 1)
    wait_head(1)
    forward_pair(1, (1, 0))
    for tile in (0, 1):
        backward_tile(1, tile)
        send_back(tile)
    forward_pair(1, (3, 2))
    for tile in (2, 3):
        backward_tile(0, tile)
        backward_tile(1, tile)
        send_back(tile)
    backward_tile(1, 8)
    send_back(4)
    backward_tile(0, 4, (0, 1))
    backward_tile(0, 5, (1,))
    for i in range(4):
        grad_queries(0, i)
    send_grad(0, range(4))
    backward_tile(1, 4)
    backward_tile(1, 5)
    grad_queries(1, 0)
    grad_queries(1, 1)
    send_grad(1, (0, 1))
    backward_tile(1, 6)
    backward_tile(1, 7)
    grad_queries(1, 2)
    grad_queries(1, 3)
    send_grad(1, (2, 3))
    for tile in range(4):
        send_sum(tile)

    @pl.loop(0, n)
    def _(other):
        for kind in range(2):
            for head in range(2):
                dst = out_dst(kind, head, other)
                pltpu.make_async_copy(dst, dst, out_rsem.at[kind, head, other]).wait()
            dst = own_dst(kind, other)
            pltpu.make_async_copy(dst, dst, own_rsem.at[kind, other]).wait()
            pl.when(has_after)(forward(kind, other).wait_send)

        @pl.when(other != h)
        def _():
            for stream in range(6):
                src = in_src(stream, other)
                pltpu.make_async_copy(src, src, in_ssem.at[stream, other]).wait()
            for kind in range(2):
                for head in range(2):
                    src = out_src(kind, head, other)
                    pltpu.make_async_copy(src, src, out_ssem.at[kind, head, other]).wait()
                src = own_buf.at[kind, other]
                pltpu.make_async_copy(src, src, own_ssem.at[kind, other]).wait()

    for side in range(2):
        for slot in range(5):
            pl.when(has_after if slot == 4 else has_before)(give_back(side, slot).wait_send)
        for piece in range(2):
            pl.when(has_before)(ahead(side, piece).wait_send)


def place_results(*refs):
    sources, places, held, sems = refs[:4], refs[4:8], refs[8:12], refs[12]
    reads = [pltpu.make_async_copy(sources[k], held[k], sems.at[0, k]) for k in range(4)]
    writes = [pltpu.make_async_copy(held[k], places[k], sems.at[1, k]) for k in range(4)]
    for read in reads:
        read.start()
    for read, write in zip(reads, writes):
        read.wait()
        write.start()
    for write in writes:
        write.wait()


def local(queries, key_rows, value_rows, grad_out, doc_start, reach_end):
    dma = pltpu.SemaphoreType.DMA
    hbm = pl.BlockSpec(memory_space=pltpu.HBM)
    results = pl.pallas_call(
        kernel,
        out_shape=[
            jax.ShapeDtypeStruct(queries.shape, bf16),
            jax.ShapeDtypeStruct(queries.shape, bf16),
            jax.ShapeDtypeStruct(key_rows.shape, bf16),
            jax.ShapeDtypeStruct(key_rows.shape, bf16),
        ],
        in_specs=[hbm] * 6,
        out_specs=[hbm, hbm, hbm, hbm],
        scratch_shapes=[
            pltpu.VMEM((4, 1, TILE), jnp.int32),
            pltpu.VMEM((4, 1, TILE), jnp.int32),
            pltpu.VMEM((2, 8, PIECE, HD), bf16),
            pltpu.VMEM((2, 8, PIECE, HD), bf16),
            pltpu.VMEM((18, PIECE, HD), bf16),
            pltpu.VMEM((18, PIECE, HD), bf16),
            pltpu.VMEM((HD, WINDOW), bf16),
            pltpu.VMEM((HD, WINDOW), bf16),
            pltpu.VMEM((2, 6, TILE, TILE), f32),
            pltpu.VMEM((2, WINDOW, BLK), bf16),
            pltpu.VMEM((2, WINDOW, BLK), bf16),
            pltpu.VMEM((2, HD, BLK), bf16),
            pltpu.VMEM((2, BLK, HD), bf16),
            pltpu.VMEM((2, BLK, HD), bf16),
            pltpu.VMEM((2, 4, 1, TILE), f32),
            pltpu.VMEM((2, 4, 1, TILE), f32),
            pltpu.VMEM((9, TILE, HD), f32),
            pltpu.VMEM((9, TILE, HD), f32),
            pltpu.VMEM((2, 8, PIECE, HD), bf16),
            pltpu.VMEM((2, 8, PIECE, HD), bf16),
            pltpu.VMEM((2, 5, TILE, HD), bf16),
            pltpu.VMEM((2, 5, TILE, HD), bf16),
            pltpu.VMEM((2, 8, PIECE, HD), bf16),
            pltpu.VMEM((PIECE, 16 * HD), bf16),
            pltpu.VMEM((PIECE, 8 * HD), bf16),
            pltpu.VMEM((PIECE, 8 * HD), bf16),
            pltpu.VMEM((PIECE, 16 * HD), bf16),
            dma((4,)),
            dma((2,)),
            dma((6, 8)),
            dma((6, 8)),
            dma((2, 8)),
            dma((2, 8)),
            dma((2, 2)),
            dma((2, 2)),
            dma((2, 2, 8)),
            dma((2, 2, 8)),
            dma((2, 5)),
            dma((2, 5)),
            dma((2, 8)),
            dma((2, 8)),
        ],
        compiler_params=pltpu.CompilerParams(
            collective_id=0, has_side_effects=True, vmem_limit_bytes=63 * 1024 * 1024
        ),
    )(
        queries, key_rows, value_rows, grad_out,
        doc_start.reshape(4, 1, TILE), reach_end.reshape(4, 1, TILE),
    )
    return pl.pallas_call(
        place_results,
        out_shape=[jax.ShapeDtypeStruct(r.shape, r.dtype) for r in results],
        in_specs=[hbm] * 4,
        out_specs=[hbm] * 4,
        scratch_shapes=[pltpu.VMEM(r.shape, r.dtype) for r in results] + [dma((2, 4))],
        compiler_params=pltpu.CompilerParams(vmem_limit_bytes=63 * 1024 * 1024),
    )(*results)


def solution(mesh):
    rows = P(("ctx", "head"), None)
    return jax.shard_map(
        local,
        mesh=mesh,
        in_specs=(rows, rows, rows, rows, P("ctx"), P("ctx")),
        out_specs=(rows, rows, rows, rows),
        check_vma=False,
    )
```

```python
import jax
import jax.numpy as jnp
from jax import lax
from jax.experimental import pallas as pl
from jax.experimental.pallas import tpu as pltpu
from jax.sharding import PartitionSpec as P

HD = 128
BLK = 1024
PIECE = 128
TILE = 256
WINDOW = 2304
SCALE = 168.0 ** (-0.5)
SCALE_LOG2 = SCALE * 1.4426950408889634
MASKED = -1e30
MESH = pl.DeviceIdType.MESH
f32 = jnp.float32
bf16 = jnp.bfloat16


def matmul(left, right):
    return lax.dot_general(left, right, (((1,), (0,)), ((), ())), preferred_element_type=f32)


def kernel(
    q_hbm, k_hbm, v_hbm, g_hbm, lower_hbm, upper_hbm,
    o_hbm, gq_hbm, gk_hbm, gv_hbm,
    lower_ref, upper_ref, q_buf, g_buf, k_win, v_win, kt_win, vt_win, s_buf, p_buf, ds_buf,
    gt_buf, gs_buf, qs_buf, delta_buf, scaled_buf, dk_acc, dv_acc,
    o_buf, gq_buf, ret_send, ret_recv, own_buf,
    q_own, k_own, v_own, g_own, stage_sem, mark_sem, in_ssem, in_rsem, fwd_ssem, fwd_rsem, ahead_ssem, ahead_rsem,
    out_ssem, out_rsem, ret_ssem, ret_rsem, own_ssem, own_rsem,
):
    n_ctx = lax.axis_size("ctx")
    n = lax.axis_size("head")
    c = lax.axis_index("ctx")
    h = lax.axis_index("head")
    after = lax.rem(c + 1, n_ctx)
    before = lax.rem(c + n_ctx - 1, n_ctx)
    has_after = c < n_ctx - 1
    has_before = c > 0

    stages = [
        pltpu.make_async_copy(src, dst, stage_sem.at[k])
        for k, (src, dst) in enumerate(
            ((k_hbm, k_own), (v_hbm, v_own), (q_hbm, q_own), (g_hbm, g_own))
        )
    ]
    for stage in stages:
        stage.start()

    barrier = pltpu.get_barrier_semaphore()

    @pl.loop(1, n)
    def _(r):
        pl.semaphore_signal(barrier, inc=1, device_id=(c, lax.rem(h + r, n)), device_id_type=MESH)

    @pl.when(has_after)
    def _():
        pl.semaphore_signal(barrier, inc=1, device_id=(after, h), device_id_type=MESH)

    @pl.when(has_before)
    def _():
        pl.semaphore_signal(barrier, inc=1, device_id=(before, h), device_id_type=MESH)

    neighbours = jnp.where(has_after, 1, 0) + jnp.where(has_before, 1, 0)
    pl.semaphore_wait(barrier, n - 1 + neighbours)

    def in_src(stream, target):
        if stream < 2:
            return (k_own, v_own)[stream].at[:, pl.ds(pl.multiple_of(target * HD, HD), HD)]
        head = (stream - 2) // 2
        cols = pl.ds(pl.multiple_of(target * 2 * HD + head * HD, HD), HD)
        return (q_own, g_own)[stream % 2].at[:, cols]

    def in_dst(stream, source):
        if stream < 2:
            return (k_win, v_win)[stream].at[8 + source]
        return (q_buf, g_buf)[stream % 2].at[(stream - 2) // 2, source]

    def send_in(streams):
        for stream in streams:
            pltpu.make_async_copy(
                in_src(stream, h), in_dst(stream, h), in_rsem.at[stream, h]
            ).start()

        @pl.loop(1, n)
        def _(r):
            target = lax.rem(h + r, n)
            for stream in streams:
                pltpu.make_async_remote_copy(
                    src_ref=in_src(stream, target),
                    dst_ref=in_dst(stream, h),
                    send_sem=in_ssem.at[stream, target],
                    recv_sem=in_rsem.at[stream, h],
                    device_id=(c, target),
                    device_id_type=MESH,
                ).start()

    def wait_in(stream, source):
        dst = in_dst(stream, source)
        pltpu.make_async_copy(dst, dst, in_rsem.at[stream, source]).wait()

    def forward(side, piece):
        win = (k_win, v_win)[side]
        return pltpu.make_async_remote_copy(
            src_ref=win.at[8 + piece],
            dst_ref=win.at[piece],
            send_sem=fwd_ssem.at[side, piece],
            recv_sem=fwd_rsem.at[side, piece],
            device_id=(after, h),
            device_id_type=MESH,
        )

    def ahead(side, piece):
        win = (k_win, v_win)[side]
        return pltpu.make_async_remote_copy(
            src_ref=win.at[8 + piece],
            dst_ref=win.at[16 + piece],
            send_sem=ahead_ssem.at[side, piece],
            recv_sem=ahead_rsem.at[side, piece],
            device_id=(before, h),
            device_id_type=MESH,
        )

    marks = [
        pltpu.make_async_copy(src, dst, mark_sem.at[k])
        for k, (src, dst) in enumerate(((lower_hbm, lower_ref), (upper_hbm, upper_ref)))
    ]
    for mark in marks:
        mark.start()
    stages[0].wait()
    stages[1].wait()

    @pl.when(has_after)
    def _():
        for side in range(2):
            pltpu.make_async_remote_copy(
                src_ref=in_src(side, h),
                dst_ref=(k_win, v_win)[side].at[h],
                send_sem=fwd_ssem.at[side, h],
                recv_sem=fwd_rsem.at[side, h],
                device_id=(after, h),
                device_id_type=MESH,
            ).start()

    send_in((0, 1))
    stages[2].wait()
    stages[3].wait()
    send_in((2, 3))
    for piece in (7, 6, 0, 1, 5, 4, 3, 2):
        for side in range(2):
            wait_in(side, piece)
            if piece >= 2:
                pl.when(has_after & (h != piece))(forward(side, piece).start)
            else:
                pl.when(has_before)(ahead(side, piece).start)

    for piece in (1, 0):
        for side in range(2):
            pl.when(has_after & (h != piece))(forward(side, piece).start)

    send_in((4, 5))

    @pl.when(jnp.logical_not(has_before))
    def _():
        for side in range(2):
            (k_win, v_win)[side][0:8] = jnp.zeros((8, PIECE, HD), bf16)
            ret_recv[side, 4] = jnp.zeros((TILE, HD), bf16)

    @pl.when(jnp.logical_not(has_after))
    def _():
        for side in range(2):
            (k_win, v_win)[side][16:18] = jnp.zeros((2, PIECE, HD), bf16)
            ret_recv[side, 0:4] = jnp.zeros((4, TILE, HD), bf16)

    for mark in marks:
        mark.wait()
    def keys(tile):
        return k_win[2 * tile : 2 * tile + 2].reshape(TILE, HD)

    def values(tile):
        return v_win[2 * tile : 2 * tile + 2].reshape(TILE, HD)

    def turn(tile):
        rows = pl.ds(tile * TILE, TILE)
        kt_win[:, rows] = keys(tile).T
        vt_win[:, rows] = values(tile).T

    for tile in range(4, 8):
        turn(tile)
    dk_acc[...] = jnp.zeros_like(dk_acc)
    dv_acc[...] = jnp.zeros_like(dv_acc)
    place = lax.broadcasted_iota(jnp.int32, (TILE, TILE), 0)

    def scores(head, i):
        rows = pl.ds(2 * i, 2)
        qt = q_buf[head, rows].reshape(TILE, HD).T
        gt_buf[head, :, pl.ds(i * TILE, TILE)] = g_buf[head, rows].reshape(TILE, HD).T
        first = (c - 1) * BLK + i * TILE
        lower = lower_ref[i] - first
        upper = upper_ref[i] - first
        top = None
        for t in range(6 if i == 3 else 5):
            s = matmul(keys(i + t), qt) * SCALE_LOG2
            allowed = place >= lower - t * TILE
            if t >= 4:
                allowed = allowed & (place <= upper - t * TILE)
            s = jnp.where(allowed, s, MASKED)
            s_buf[i % 2, t] = s
            most = jnp.max(s, axis=0, keepdims=True)
            top = most if top is None else jnp.maximum(top, most)
        return top

    def attend(head, i, top):
        tiles = 6 if i == 3 else 5
        rows = pl.ds(2 * i, 2)
        lanes = pl.ds(i * TILE, TILE)
        window = pl.ds(i * TILE, tiles * TILE)
        total = None
        for t in range(tiles):
            p = jnp.exp2(s_buf[i % 2, t] - top)
            p_buf[head, pl.ds((i + t) * TILE, TILE), lanes] = p.astype(bf16)
            part = jnp.sum(p, axis=0, keepdims=True)
            total = part if total is None else total + part
        share = 1.0 / total
        out = (matmul(vt_win[:, window], p_buf[head, window, lanes]) * share).astype(bf16)
        o_buf[head, rows] = out.T.reshape(2, PIECE, HD)
        gt = gt_buf[head, :, lanes].astype(f32)
        delta_buf[head, i] = jnp.sum(gt * out.astype(f32), axis=0, keepdims=True)
        scaled_buf[head, i] = share * SCALE
        column = jnp.broadcast_to(share, (8, TILE)).T[:, :1]
        g = g_buf[head, rows].reshape(TILE, HD).astype(f32)
        q = q_buf[head, rows].reshape(TILE, HD).astype(f32)
        gs_buf[head, lanes] = (g * column).astype(bf16)
        qs_buf[head, lanes] = (q * (column * SCALE)).astype(bf16)

    def backward_tile(head, tile, blocks=range(4)):
        reach = range(max(0, tile - 4), 1 + min(3, tile)) if tile < 8 else range(3, 4)
        blocks = [i for i in reach if i in blocks]
        rows = pl.ds(tile * TILE, TILE)
        span = pl.ds(blocks[0] * TILE, len(blocks) * TILE)
        v = values(tile)
        dv_acc[tile] += matmul(p_buf[head, rows, span], gs_buf[head, span])
        for i in blocks:
            lanes = pl.ds(i * TILE, TILE)
            dp = matmul(v, gt_buf[head, :, lanes])
            ds_buf[head, rows, lanes] = p_buf[head, rows, lanes] * (
                dp - delta_buf[head, i]
            ).astype(bf16)
        dk_acc[tile] += matmul(ds_buf[head, rows, span], qs_buf[head, span])

    def grad_queries(head, i):
        lanes = pl.ds(i * TILE, TILE)
        window = pl.ds(i * TILE, (6 if i == 3 else 5) * TILE)
        grad = matmul(kt_win[:, window], ds_buf[head, window, lanes]) * scaled_buf[head, i]
        gq_buf[head, pl.ds(2 * i, 2)] = grad.astype(bf16).T.reshape(2, PIECE, HD)

    def out_src(kind, head, target):
        return (o_buf, gq_buf)[kind].at[head, target]

    def out_dst(kind, head, source):
        cols = pl.ds(pl.multiple_of(source * 2 * HD + head * HD, HD), HD)
        return (o_hbm, gq_hbm)[kind].at[:, cols]

    def send_out(kind, head, target):
        @pl.when(target == h)
        def _():
            pltpu.make_async_copy(
                out_src(kind, head, target), out_dst(kind, head, h), out_rsem.at[kind, head, h]
            ).start()

        @pl.when(target != h)
        def _():
            pltpu.make_async_remote_copy(
                src_ref=out_src(kind, head, target),
                dst_ref=out_dst(kind, head, h),
                send_sem=out_ssem.at[kind, head, target],
                recv_sem=out_rsem.at[kind, head, h],
                device_id=(c, target),
                device_id_type=MESH,
            ).start()

    def give_back(side, slot):
        return pltpu.make_async_remote_copy(
            src_ref=ret_send.at[side, slot],
            dst_ref=ret_recv.at[side, slot],
            send_sem=ret_ssem.at[side, slot],
            recv_sem=ret_rsem.at[side, slot],
            device_id=(after if slot == 4 else before, h),
            device_id_type=MESH,
        )

    def own_dst(side, source):
        return (gk_hbm, gv_hbm)[side].at[:, pl.ds(pl.multiple_of(source * HD, HD), HD)]

    def send_own(side, target):
        @pl.when(target == h)
        def _():
            pltpu.make_async_copy(
                own_buf.at[side, target], own_dst(side, h), own_rsem.at[side, h]
            ).start()

        @pl.when(target != h)
        def _():
            pltpu.make_async_remote_copy(
                src_ref=own_buf.at[side, target],
                dst_ref=own_dst(side, h),
                send_sem=own_ssem.at[side, target],
                recv_sem=own_rsem.at[side, h],
                device_id=(c, target),
                device_id_type=MESH,
            ).start()

    def send_sum(tile):
        @pl.when(has_after)
        def _():
            for side in range(2):
                give_back(side, tile).wait_recv()

        if tile == 0:
            @pl.when(has_before)
            def _():
                for side in range(2):
                    give_back(side, 4).wait_recv()

        for side in range(2):
            acc = (dk_acc, dv_acc)[side]
            total = acc[4 + tile] + ret_recv[side, tile].astype(f32)
            if tile == 0:
                total += ret_recv[side, 4].astype(f32)
            own_buf[side, 2 * tile : 2 * tile + 2] = total.astype(bf16).reshape(2, PIECE, HD)
            for part in range(2):
                send_own(side, 2 * tile + part)

    def send_back(slot):
        tile = 8 if slot == 4 else slot
        for side in range(2):
            ret_send[side, slot] = (dk_acc, dv_acc)[side][tile].astype(bf16)
            pl.when(has_after if slot == 4 else has_before)(give_back(side, slot).start)

    def wait_head(head):
        @pl.loop(0, n)
        def _(source):
            for kind in range(2):
                wait_in(2 + 2 * head + kind, source)

    def wait_prior(tiles):
        @pl.when(has_before)
        def _():
            for tile in tiles:
                for piece in (2 * tile, 2 * tile + 1):
                    for side in range(2):
                        forward(side, piece).wait_recv()

        for tile in tiles:
            turn(tile)

    def forward_pair(head, pair):
        tops = [scores(head, i) for i in pair]
        for i, top in zip(pair, tops):
            attend(head, i, top)
        for i in pair:
            for part in range(2):
                send_out(0, head, 2 * i + part)

    def send_grad(head, blocks):
        for i in blocks:
            for part in range(2):
                send_out(1, head, 2 * i + part)

    wait_head(0)
    wait_prior((3, 2))

    @pl.when(has_after)
    def _():
        for piece in range(2):
            for side in range(2):
                ahead(side, piece).wait_recv()

    turn(8)
    forward_pair(0, (3, 2))
    for tile in (8, 4, 5, 6, 7):
        backward_tile(0, tile, (2, 3))
    wait_prior((1, 0))
    forward_pair(0, (1, 0))
    backward_tile(0, 0)
    backward_tile(0, 1)
    wait_head(1)
    for tile in (0, 1):
        forward_pair(1, (tile,))
        backward_tile(1, tile)
        send_back(tile)
    forward_pair(1, (3, 2))
    for tile in (2, 3):
        backward_tile(0, tile)
        backward_tile(1, tile)
        send_back(tile)
    backward_tile(1, 8)
    send_back(4)
    backward_tile(0, 4, (0, 1))
    backward_tile(0, 5, (1,))
    for i in range(4):
        grad_queries(0, i)
    send_grad(0, range(4))
    backward_tile(1, 4)
    backward_tile(1, 5)
    grad_queries(1, 0)
    grad_queries(1, 1)
    send_grad(1, (0, 1))
    send_sum(1)
    backward_tile(1, 6)
    backward_tile(1, 7)
    grad_queries(1, 2)
    grad_queries(1, 3)
    send_grad(1, (2, 3))
    for tile in (0, 2, 3):
        send_sum(tile)

    @pl.loop(0, n)
    def _(other):
        for kind in range(2):
            for head in range(2):
                dst = out_dst(kind, head, other)
                pltpu.make_async_copy(dst, dst, out_rsem.at[kind, head, other]).wait()
            dst = own_dst(kind, other)
            pltpu.make_async_copy(dst, dst, own_rsem.at[kind, other]).wait()
            pl.when(has_after)(forward(kind, other).wait_send)

        @pl.when(other != h)
        def _():
            for stream in range(6):
                src = in_src(stream, other)
                pltpu.make_async_copy(src, src, in_ssem.at[stream, other]).wait()
            for kind in range(2):
                for head in range(2):
                    src = out_src(kind, head, other)
                    pltpu.make_async_copy(src, src, out_ssem.at[kind, head, other]).wait()
                src = own_buf.at[kind, other]
                pltpu.make_async_copy(src, src, own_ssem.at[kind, other]).wait()

    for side in range(2):
        for slot in range(5):
            pl.when(has_after if slot == 4 else has_before)(give_back(side, slot).wait_send)
        for piece in range(2):
            pl.when(has_before)(ahead(side, piece).wait_send)


def place_results(*refs):
    sources, places, held, sems = refs[:4], refs[4:8], refs[8:12], refs[12]
    reads = [pltpu.make_async_copy(sources[k], held[k], sems.at[0, k]) for k in range(4)]
    writes = [pltpu.make_async_copy(held[k], places[k], sems.at[1, k]) for k in range(4)]
    for read in reads:
        read.start()
    for read, write in zip(reads, writes):
        read.wait()
        write.start()
    for write in writes:
        write.wait()


def local(queries, key_rows, value_rows, grad_out, doc_start, reach_end):
    dma = pltpu.SemaphoreType.DMA
    hbm = pl.BlockSpec(memory_space=pltpu.HBM)
    results = pl.pallas_call(
        kernel,
        out_shape=[
            jax.ShapeDtypeStruct(queries.shape, bf16),
            jax.ShapeDtypeStruct(queries.shape, bf16),
            jax.ShapeDtypeStruct(key_rows.shape, bf16),
            jax.ShapeDtypeStruct(key_rows.shape, bf16),
        ],
        in_specs=[hbm] * 6,
        out_specs=[hbm, hbm, hbm, hbm],
        scratch_shapes=[
            pltpu.VMEM((4, 1, TILE), jnp.int32),
            pltpu.VMEM((4, 1, TILE), jnp.int32),
            pltpu.VMEM((2, 8, PIECE, HD), bf16),
            pltpu.VMEM((2, 8, PIECE, HD), bf16),
            pltpu.VMEM((18, PIECE, HD), bf16),
            pltpu.VMEM((18, PIECE, HD), bf16),
            pltpu.VMEM((HD, WINDOW), bf16),
            pltpu.VMEM((HD, WINDOW), bf16),
            pltpu.VMEM((2, 6, TILE, TILE), f32),
            pltpu.VMEM((2, WINDOW, BLK), bf16),
            pltpu.VMEM((2, WINDOW, BLK), bf16),
            pltpu.VMEM((2, HD, BLK), bf16),
            pltpu.VMEM((2, BLK, HD), bf16),
            pltpu.VMEM((2, BLK, HD), bf16),
            pltpu.VMEM((2, 4, 1, TILE), f32),
            pltpu.VMEM((2, 4, 1, TILE), f32),
            pltpu.VMEM((9, TILE, HD), f32),
            pltpu.VMEM((9, TILE, HD), f32),
            pltpu.VMEM((2, 8, PIECE, HD), bf16),
            pltpu.VMEM((2, 8, PIECE, HD), bf16),
            pltpu.VMEM((2, 5, TILE, HD), bf16),
            pltpu.VMEM((2, 5, TILE, HD), bf16),
            pltpu.VMEM((2, 8, PIECE, HD), bf16),
            pltpu.VMEM((PIECE, 16 * HD), bf16),
            pltpu.VMEM((PIECE, 8 * HD), bf16),
            pltpu.VMEM((PIECE, 8 * HD), bf16),
            pltpu.VMEM((PIECE, 16 * HD), bf16),
            dma((4,)),
            dma((2,)),
            dma((6, 8)),
            dma((6, 8)),
            dma((2, 8)),
            dma((2, 8)),
            dma((2, 2)),
            dma((2, 2)),
            dma((2, 2, 8)),
            dma((2, 2, 8)),
            dma((2, 5)),
            dma((2, 5)),
            dma((2, 8)),
            dma((2, 8)),
        ],
        compiler_params=pltpu.CompilerParams(
            collective_id=0, has_side_effects=True, vmem_limit_bytes=63 * 1024 * 1024
        ),
    )(
        queries, key_rows, value_rows, grad_out,
        doc_start.reshape(4, 1, TILE), reach_end.reshape(4, 1, TILE),
    )
    return pl.pallas_call(
        place_results,
        out_shape=[jax.ShapeDtypeStruct(r.shape, r.dtype) for r in results],
        in_specs=[hbm] * 4,
        out_specs=[hbm] * 4,
        scratch_shapes=[pltpu.VMEM(r.shape, r.dtype) for r in results] + [dma((2, 4))],
        compiler_params=pltpu.CompilerParams(vmem_limit_bytes=63 * 1024 * 1024),
    )(*results)


def solution(mesh):
    rows = P(("ctx", "head"), None)
    return jax.shard_map(
        local,
        mesh=mesh,
        in_specs=(rows, rows, rows, rows, P("ctx"), P("ctx")),
        out_specs=(rows, rows, rows, rows),
        check_vma=False,
    )
```
